512 devices in a mesh: blk: 16 (over y_lo, x), band: 32 (over y_hi, z, core).
Axes of the slice: x: 4, y: 8 (y_hi: 2, y_lo: 4; y = y_hi * 4 + y_lo), z: 8, core: 2. Of those that a mesh axis runs over, the one named last changes fastest.
Arguments:
- fine_blocks: float32 [2048, 64, 256], P(('blk', 'band')), may hold values from -3 to 3
- source_group: int32 [2048, 4], P(('blk', 'band')), may hold values from 0 to 15, all different within a row; in each aligned block of 4 rows (0 to 3, 4 to 7, ...) at most 2 rows name the same one
- source_row: int32 [2048, 4], P(('blk', 'band')), may hold values from 0 to 3
- prolong_blocks: float32 [2048, 64, 128], P(('blk', 'band')), may hold values from -0.75 to 0.75
- prolong_code: int32 [2048, 2], P(('blk', 'band')), may hold values from 0 to 2
Outputs:
- coarse_rows: float32 [32768, 5120], P(('blk', 'band'))
The draws below stay inside these ranges and needn't reach their ends.
Inputs may be any that keep to these rules, and one draw needn't show every extreme that they name: `source_group`: each fine block row names 4 different groups; among the rows of one device no group is named more than 2 times, and some device names one group exactly 2 times.
All inputs are finite; a program needn't handle non-finite values.
Results may differ from the reference program's by a relative error of at most 0.0003.
Values sent between devices are 32-bit elements; how exact they have to be, the bound alone decides.
A program may use at most 64 MiB of HBM per device.

```python
import math
import jax
import jax.numpy as jnp
import numpy as np
from jax import lax

B = 64
FB = 4
KA = 4
KP = 2
CB = 1
MB = 2
NF = 2048
N_BLK = 16
N_BAND = 32


def place_ends(values, key, smallest, largest):
    index_at = [jax.random.randint(jax.random.fold_in(key, axis), (), 0, length) for axis, length in enumerate(values.shape)]
    widest = values.shape.index(max(values.shape))
    neighbour = index_at[:widest] + [(index_at[widest] + 1) % values.shape[widest]] + index_at[widest + 1:]
    return values.at[tuple(index_at)].set(smallest).at[tuple(neighbour)].set(largest)


def level_of(key, extent, pieces, smallest, largest):
    factor_of, own = 1.0, jax.random.fold_in(key, 6)
    for axis_at, parts in pieces:
        steps = jnp.exp(jax.random.uniform(jax.random.fold_in(own, axis_at), (parts,), jnp.float32, smallest / len(pieces), largest / len(pieces)))
        factor_of = factor_of * jnp.repeat(steps, extent[axis_at] // parts).reshape([-1 if axis == axis_at else 1 for axis in range(len(extent))])
    return factor_of


def routed_block(rng, own, number, rows, count, top, bound, lean):
    sequence = jax.random.permutation(rng, count)
    crowded, usual = portions_of(count, rows * top, bound, lean, True), portions_of(count, rows * top, bound, lean, False)
    places = jnp.arange(count)

    def named(tallies, turn):
        used = int((tallies > 0).sum())
        fixed = max(1, used // 4)
        shifted = fixed + (places - fixed + turn * (used - fixed)) % max(1, count - fixed)
        return jnp.zeros((count,), jnp.int32).at[sequence[jnp.where(places < fixed, places, shifted)]].set(jnp.asarray(tallies, jnp.int32))

    tallies = jnp.where(number % 4 == 0, named(crowded, number // 4), named(usual, number - number // 4 - 1))
    mixed = jax.random.permutation(jax.random.fold_in(own, 3), count)
    giver, taker = mixed[0:count // 2 * 2:2], mixed[1:count // 2 * 2:2]
    margin = jnp.minimum(tallies[giver] - 1, bound - tallies[taker]) // 2
    margin = jnp.where((giver == sequence[0]) | (taker == sequence[0]) | (tallies[taker] == 0), 0, jnp.maximum(margin, 0))
    shifted = jax.random.randint(jax.random.fold_in(own, 4), (count // 2,), 0, 1 << 20) % (margin + 1)
    tallies = tallies.at[giver].add(-shifted).at[taker].add(shifted)
    members = jnp.searchsorted(jnp.cumsum(tallies), jnp.arange(rows * top), side="right").astype(jnp.int32)
    table = members.reshape(top, rows).T
    table = table[jax.random.permutation(jax.random.fold_in(own, 1), rows)]
    turn = jax.random.randint(jax.random.fold_in(own, 2), (rows, 1), 0, top)
    return jnp.take_along_axis(table, (jnp.arange(top)[None, :] + turn) % top, axis=1)


def portions_of(number_of, total, most, skew, full):
    portions = [(1 << 20) // math.isqrt(rank ** skew) + 1 for rank in range(1, number_of + 1)]
    largest = most if full else min(most, max(-(-total // number_of), total * portions[0] // sum(portions)))
    least = 1 if total - largest >= number_of - 1 else 0
    given, spare = [largest] + [least] * (number_of - 1), total - largest - least * (number_of - 1)
    while spare > 0:
        free = [i for i in range(1, number_of) if given[i] < largest] or [i for i in range(1, number_of) if given[i] < most]
        whole, left = sum([portions[i] for i in free]), spare
        for i in free:
            more = min(most - given[i], max(1, left * portions[i] // whole), spare)
            given[i] = given[i] + more
            spare = spare - more
    return np.array(given)


def noise(own_key, dims, deviation, reach, pieces=(), kind=jnp.bfloat16):
    entries = jax.random.normal(own_key, dims, jnp.float32) * deviation
    if len(pieces) > 0:
        entries = level_of(own_key, dims, pieces, -0.22, 0.18) * entries
    return jnp.clip(entries, min=-reach, max=reach).astype(kind)


def setup_inputs(seed: int = 0) -> dict:
    keys = jax.random.split(jax.random.key(seed), 6)
    fine_blocks = noise(keys[0], (NF, B, KA * B), 0.5, 3.0, ((0, 512),), jnp.float32)
    source_group_keys = jax.random.split(jax.random.fold_in(keys[1], 1), NF // FB)
    source_group_turns = jax.random.permutation(jax.random.fold_in(keys[1], 3), NF // FB)
    source_group = jax.vmap(lambda own, number: routed_block(jax.random.fold_in(keys[1], 2), own, number, FB, N_BLK, KA, MB, 2))(source_group_keys, source_group_turns).reshape((NF, KA))
    source_row = place_ends(jax.random.randint(keys[2], (NF, KA), 0, FB), jax.random.fold_in(keys[2], 1), 0, FB - 1).astype(jnp.int32)
    prolong_blocks = noise(keys[3], (NF, B, KP * B), B ** -0.5, 0.75, ((0, 512),), jnp.float32)
    prolong_code = place_ends(jax.random.randint(keys[4], (NF, KP), 0, 3 * CB), jax.random.fold_in(keys[4], 1), 0, (3 * CB) - 1).astype(jnp.int32)
    return {"fine_blocks": fine_blocks, "source_group": source_group, "source_row": source_row, "prolong_blocks": prolong_blocks, "prolong_code": prolong_code}


def reference(fine_blocks, source_group, source_row, prolong_blocks, prolong_code):
    devices_all = N_BLK * N_BAND
    fine_total = FB * devices_all
    window_blocks = 5 * N_BLK * CB
    a_tiles = fine_blocks.reshape(fine_total, B, KA, B).transpose(0, 2, 1, 3)
    p_tiles = prolong_blocks.reshape(fine_total, B, KP, B)
    coarse = jnp.zeros((CB * devices_all, B, window_blocks, B), jnp.float32)

    def one_device(coarse, device):
        group_id = device // N_BAND
        band_id = device % N_BAND
        first_row = device * FB
        a_here = lax.dynamic_slice_in_dim(a_tiles, first_row, FB, 0)
        p_here = lax.dynamic_slice_in_dim(p_tiles, first_row, FB, 0)
        code_here = lax.dynamic_slice_in_dim(prolong_code, first_row, FB, 0)
        group_here = lax.dynamic_slice_in_dim(source_group, first_row, FB, 0)
        row_here = lax.dynamic_slice_in_dim(source_row, first_row, FB, 0)
        source = (group_here * N_BAND + band_id) * FB + row_here
        p_source = p_tiles[source]
        code_source = prolong_code[source]
        left_part = jnp.einsum("ianx,ikab->inkxb", p_here, a_here, precision=lax.Precision.HIGHEST)
        products = jnp.einsum("inkxb,ikbmy->inkmxy", left_part, p_source, precision=lax.Precision.HIGHEST)
        shift_n = code_here // CB
        slot_n = code_here % CB
        shift_m = code_source // CB
        slot_m = code_source % CB
        owner_device = group_id * N_BAND + (band_id + shift_n - 1) % N_BAND
        row_block = owner_device * CB + slot_n
        offset = shift_m[:, None, :, :] - shift_n[:, :, None, None] + 2
        col_block = (offset * N_BLK + group_here[:, None, :, None]) * CB + slot_m[:, None, :, :]
        row_all = jnp.broadcast_to(row_block[:, :, None, None], col_block.shape)
        coarse = coarse.at[row_all.reshape(-1), :, col_block.reshape(-1), :].add(products.reshape(-1, B, B))
        return coarse, None

    coarse, unused_out = lax.scan(one_device, coarse, jnp.arange(devices_all, dtype=jnp.int32))
    return coarse.reshape(CB * devices_all * B, window_blocks * B)
```

```python
import jax
import jax.numpy as jnp
from jax import lax
from jax.experimental import pallas as pl
from jax.experimental.pallas import tpu as pltpu
from jax.sharding import PartitionSpec as P

MESH = pl.DeviceIdType.MESH
F32 = jnp.float32
BF16 = jnp.bfloat16

B = 64
FB = 4
KA = 4
NX = 4
NY = 4
PACK = FB * B + 8
HEAD = 136
STEPS = NX * NY // 2


def kernel(
    a_ref, p_ref, group_ref, row_ref, code_ref, out_ref,
    held, left_hi, left_lo, win_hi, win_lo, middle, up_out, down_out, lower, upper,
    pair_tab, row_tab,
    y_send, y_recv, x_send, x_recv, h_send, h_recv, halo_send, halo_recv,
):
    blk, band = lax.axis_index("blk"), lax.axis_index("band")
    bands = lax.axis_size("band")
    y, x = blk // NX, blk % NX
    right, left = (x + 1) % NX, (x + NX - 1) % NX
    above, below = (band + 1) % bands, (band + bands - 1) % bands
    lane = lax.broadcasted_iota(jnp.int32, (B, 2 * B), 1)
    first_half = lane < B

    def at(row, column):
        return (row * NX + column, band)

    barrier = pltpu.get_barrier_semaphore()
    for target in (at(y, right), at(y, left), (blk, above), (blk, below)):
        pl.semaphore_signal(barrier, inc=1, device_id=target, device_id_type=MESH)

    @pl.when(y < NY - 1)
    def _():
        pl.semaphore_signal(barrier, inc=1, device_id=at(y + 1, x), device_id_type=MESH)

    @pl.when(y > 0)
    def _():
        pl.semaphore_signal(barrier, inc=1, device_id=at(y - 1, x), device_id_type=MESH)

    held[blk, 0 : FB * B, :] = p_ref[...].reshape(FB * B, 2 * B)
    tile_row = lax.broadcasted_iota(jnp.int32, (8, 2 * B), 0)
    tile_lane = lax.broadcasted_iota(jnp.int32, (8, 2 * B), 1)
    codes = jnp.zeros((8, 2 * B), F32)
    for i in range(FB):
        one = jnp.where(tile_lane < B, code_ref[i, 0], code_ref[i, 1]).astype(F32)
        codes = jnp.where(tile_row == i, one, codes)
    held[blk, FB * B : PACK, :] = codes

    pl.semaphore_wait(barrier, 4 + jnp.where(y < NY - 1, 1, 0) + jnp.where(y > 0, 1, 0))

    def y_copy(source, target, sender):
        slot = held.at[source * NX + x]
        return pltpu.make_async_remote_copy(
            src_ref=slot, dst_ref=slot, send_sem=y_send.at[sender], recv_sem=y_recv.at[source],
            device_id=at(target, x), device_id_type=MESH,
        )

    def x_copy(source, column, side):
        slot = held.at[source * NX + column]
        return pltpu.make_async_remote_copy(
            src_ref=slot, dst_ref=slot, send_sem=x_send.at[side, source], recv_sem=x_recv.at[side, source],
            device_id=at(y, left if side else right), device_id_type=MESH,
        )

    def h_copy(source, column, side):
        rows = pl.ds(HEAD, PACK - HEAD) if side else pl.ds(0, HEAD)
        slot = held.at[source * NX + column, rows]
        return pltpu.make_async_remote_copy(
            src_ref=slot, dst_ref=slot, send_sem=h_send.at[side, source], recv_sem=h_recv.at[side, source],
            device_id=at(y, left if side else right), device_id_type=MESH,
        )

    def halo_copy(step, side):
        return pltpu.make_async_remote_copy(
            src_ref=(down_out if side else up_out).at[step], dst_ref=(upper if side else lower).at[step],
            send_sem=halo_send.at[side, step], recv_sem=halo_recv.at[side, step],
            device_id=(blk, below if side else above), device_id_type=MESH,
        )

    order = [
        y,
        jnp.where(y == 0, 1, y - 1),
        jnp.where(y == 0, 2, jnp.where(y == 3, 1, y + 1)),
        jnp.where(y < 2, 3, 0),
    ]

    def onward(source):
        return jnp.where(source < y, y + 1, y - 1)

    def inside(target):
        return (target >= 0) & (target < NY)

    def x_start(source):
        x_copy(source, x, 0).start()
        x_copy(source, x, 1).start()

    def y_take(turn):
        source = order[turn]
        y_copy(source, jnp.where(source < y, y - 1, y + 1), 1 + turn).wait_recv()
        target = onward(source)

        @pl.when(inside(target))
        def _():
            y_copy(source, target, 1 + turn).start()

        x_start(source)

    def x_take(turn):
        source = order[turn]
        x_copy(source, left, 0).wait_recv()
        h_copy(source, left, 0).start()
        x_copy(source, right, 1).wait_recv()
        h_copy(source, right, 1).start()

    def h_take(turn):
        source = order[turn]
        far = (x + 2) % NX
        h_copy(source, far, 0).wait_recv()
        h_copy(source, far, 1).wait_recv()

    @pl.when(y < NY - 1)
    def _():
        y_copy(y, y + 1, 0).start()

    @pl.when(y > 0)
    def _():
        y_copy(y, y - 1, 1).start()

    x_start(y)

    def tabulate(group, carry):
        pair = [jnp.int32(0), jnp.int32(0)]
        row = [jnp.int32(FB), jnp.int32(FB)]
        for at_pair in range(FB * KA - 1, -1, -1):
            i, k = at_pair // KA, at_pair % KA
            hit = group_ref[i, k] == group
            pair = [jnp.where(hit, at_pair, pair[0]), jnp.where(hit, pair[0], pair[1])]
            row = [jnp.where(hit, row_ref[i, k], row[0]), jnp.where(hit, row[0], row[1])]
        for slot in range(2):
            pair_tab[2 * group + slot] = pair[slot]
            row_tab[2 * group + slot] = row[slot]
        return carry

    lax.fori_loop(0, NX * NY, tabulate, 0)

    def windowed(values, code, at_code):
        chosen = jnp.where(code == at_code, values, 0.0)
        return chosen + pltpu.roll(chosen, B, 1)

    def left_product(i, carry):
        p_here = p_ref[i]
        code = jnp.broadcast_to(held[blk, pl.ds(FB * B + i, 1), :], (B, 2 * B)).astype(jnp.int32)
        parts = [windowed(p_here, code, d) for d in range(3)]
        restrict = jnp.concatenate(
            [jnp.where(first_half, parts[0], parts[1]), jnp.where(first_half, parts[2], 0.0)], axis=1
        )
        twice = []
        for side in range(2):
            both = a_ref[i, :, side * 2 * B : (side + 1) * 2 * B]
            turned = pltpu.roll(both, B, 1)
            twice += [jnp.where(first_half, both, turned), jnp.where(first_half, turned, both)]
        result = lax.dot_general(
            restrict, jnp.concatenate(twice, axis=1), (((0,), (0,)), ((), ())),
            precision=lax.Precision.HIGHEST, preferred_element_type=F32,
        )[0 : 3 * B]
        high = result.astype(BF16)
        low = (result - high.astype(F32)).astype(BF16)
        for k in range(KA):
            left_hi[i * KA + k] = high[:, k * 2 * B : (k + 1) * 2 * B]
            left_lo[i * KA + k] = low[:, k * 2 * B : (k + 1) * 2 * B]
        return carry

    lax.fori_loop(0, FB, left_product, 0)

    wide_half = lax.broadcasted_iota(jnp.int32, (3 * B, 2 * B), 1) < B

    def compute(step):
        for half in range(2):
            group = 2 * step + half
            here = [held[group, i * B : (i + 1) * B, :] for i in range(FB)]
            tile = held[group, FB * B : PACK, :]
            for slot in range(2):
                row = row_tab[2 * group + slot]
                picks = [jnp.where(row == i, 1.0, 0.0).astype(F32) for i in range(FB)]
                values = sum(picks[i] * here[i] for i in range(FB))
                code = sum(picks[i] * tile[i : i + 1, :] for i in range(FB))
                code = jnp.broadcast_to(code, (B, 2 * B)).astype(jnp.int32)
                mine = first_half if half == 0 else jnp.logical_not(first_half)
                at_row = (2 * half + slot) * B
                for e in range(3):
                    part = jnp.where(mine, windowed(values, code, e), 0.0)
                    high = part.astype(BF16)
                    win_hi[at_row : at_row + B, e * 2 * B : (e + 1) * 2 * B] = high
                    win_lo[at_row : at_row + B, e * 2 * B : (e + 1) * 2 * B] = (part - high.astype(F32)).astype(BF16)

        def stacked(ref):
            pairs = [ref[pair_tab[4 * step + n]] for n in range(4)]
            return jnp.concatenate(
                [jnp.where(wide_half, pairs[0], pairs[1]), jnp.where(wide_half, pairs[2], pairs[3])], axis=1
            )

        high, low = stacked(left_hi), stacked(left_lo)
        total = jnp.dot(high, win_hi[...], preferred_element_type=F32)
        total += jnp.dot(high, win_lo[...], preferred_element_type=F32)
        total += jnp.dot(low, win_hi[...], preferred_element_type=F32)
        down_out[step] = total[0:B]
        middle[step] = total[B : 2 * B]
        up_out[step] = total[2 * B : 3 * B]
        halo_copy(step, 0).start()
        halo_copy(step, 1).start()

    def finish(step):
        halo_copy(step, 0).wait_recv()
        halo_copy(step, 1).wait_recv()
        for e in range(5):
            parts = []
            for ref, shift in ((lower, 0), (middle, 1), (upper, 2)):
                if 0 <= e - shift < 3:
                    parts.append(ref[step, :, (e - shift) * 2 * B : (e - shift + 1) * 2 * B])
            column = pl.multiple_of(e * NX * NY * B + step * 2 * B, 2 * B)
            out_ref[:, pl.ds(column, 2 * B)] = sum(parts[1:], parts[0])

    def both_steps(work, turn):
        def one(n, carry):
            work(2 * order[turn] + n)
            return carry

        lax.fori_loop(0, 2, one, 0)

    y_take(1)
    x_take(0)
    y_take(2)
    h_take(0)
    both_steps(compute, 0)
    x_take(1)
    y_take(3)
    x_take(2)
    h_take(1)
    both_steps(compute, 1)
    x_take(3)
    h_take(2)
    both_steps(compute, 2)
    both_steps(finish, 0)
    h_take(3)
    both_steps(compute, 3)
    for turn in range(1, 4):
        both_steps(finish, turn)

    @pl.when(y < NY - 1)
    def _():
        y_copy(y, y + 1, 0).wait_send()

    @pl.when(y > 0)
    def _():
        y_copy(y, y - 1, 1).wait_send()

    for turn in range(1, 4):
        target = onward(order[turn])

        @pl.when(inside(target))
        def _():
            y_copy(order[turn], target, 1 + turn).wait_send()

    def drain_x(source, carry):
        for side, column in ((0, left), (1, right)):
            x_copy(source, x, side).wait_send()
            h_copy(source, column, side).wait_send()
        return carry

    lax.fori_loop(0, NY, drain_x, 0)

    def drain_halo(step, carry):
        halo_copy(step, 0).wait_send()
        halo_copy(step, 1).wait_send()
        return carry

    lax.fori_loop(0, STEPS, drain_halo, 0)


def body(fine_blocks, source_group, source_row, prolong_blocks, prolong_code):
    vmem = pl.BlockSpec(memory_space=pltpu.VMEM)
    smem = pl.BlockSpec(memory_space=pltpu.SMEM)
    window = 3 * 2 * B
    halo = pltpu.VMEM((STEPS, B, window), F32)
    dma = pltpu.SemaphoreType.DMA
    return pl.pallas_call(
        kernel,
        out_shape=jax.ShapeDtypeStruct((B, 5 * NX * NY * B), F32),
        in_specs=[vmem, vmem, smem, smem, smem],
        out_specs=vmem,
        scratch_shapes=[
            pltpu.VMEM((NX * NY, PACK, 2 * B), F32),
            pltpu.VMEM((FB * KA, 3 * B, 2 * B), BF16),
            pltpu.VMEM((FB * KA, 3 * B, 2 * B), BF16),
            pltpu.VMEM((4 * B, window), BF16),
            pltpu.VMEM((4 * B, window), BF16),
            halo, halo, halo, halo, halo,
            pltpu.SMEM((2 * NX * NY,), jnp.int32),
            pltpu.SMEM((2 * NX * NY,), jnp.int32),
            dma((5,)), dma((NY,)),
            dma((2, NY)), dma((2, NY)),
            dma((2, NY)), dma((2, NY)),
            dma((2, STEPS)), dma((2, STEPS)),
        ],
        compiler_params=pltpu.CompilerParams(
            collective_id=0, has_side_effects=True, vmem_limit_bytes=40 * 2**20
        ),
        cost_estimate=pl.CostEstimate(flops=10**9, bytes_accessed=4 * 2**20, transcendentals=0),
        name="galerkin",
    )(fine_blocks, prolong_blocks, source_group, source_row, prolong_code)


def solution(mesh):
    return jax.shard_map(
        body,
        mesh=mesh,
        in_specs=(
            P(("blk", "band"), None, None),
            P(("blk", "band"), None),
            P(("blk", "band"), None),
            P(("blk", "band"), None, None),
            P(("blk", "band"), None),
        ),
        out_specs=P(("blk", "band"), None),
        check_vma=False,
    )
```

```python
import jax
import jax.numpy as jnp
from jax import lax
from jax.experimental import pallas as pl
from jax.experimental.pallas import tpu as pltpu
from jax.sharding import PartitionSpec as P

MESH = pl.DeviceIdType.MESH
F32 = jnp.float32
BF16 = jnp.bfloat16

B = 64
FB = 4
KA = 4
MB = 2
NX = 4
NY = 4
PACK = FB * B + 8
SHARE = MB * B + 8
STEPS = NX * NY // 2


def kernel(
    a_hbm, p_hbm, group_hbm, row_hbm, code_hbm, out_ref,
    a_ref, group_ref, row_ref, code_ref,
    held, want, asked, staged, got, left_hi, left_lo, win_hi, win_lo,
    middle, up_out, down_out, lower, upper, pair_tab,
    in_sem, y_send, y_recv, ask_send, ask_recv, x_send, x_recv, halo_send, halo_recv, ready,
):
    blk, band = lax.axis_index("blk"), lax.axis_index("band")
    bands = lax.axis_size("band")
    half_bands = bands // 2
    y, x = blk // NX, blk % NX
    above, below = (band + 1) % bands, (band + bands - 1) % bands
    is_first, is_last = band % half_bands == 0, band % half_bands == half_bands - 1
    lane = lax.broadcasted_iota(jnp.int32, (B, 2 * B), 1)
    first_half = lane < B

    def at(row, column):
        return (row * NX + column, band)

    def beside(shift):
        return (x + shift) % NX

    def signal(semaphore, target):
        pl.semaphore_signal(semaphore, inc=1, device_id=target, device_id_type=MESH)

    inputs = [
        pltpu.make_async_copy(source, target, in_sem.at[n])
        for n, (source, target) in enumerate((
            (group_hbm, group_ref), (row_hbm, row_ref), (code_hbm, code_ref),
            (p_hbm, held.at[y, pl.ds(0, FB * B)]), (a_hbm, a_ref),
        ))
    ]
    for copy in inputs:
        copy.start()

    barrier = pltpu.get_barrier_semaphore()
    for shift in range(1, NX):
        signal(barrier, at(y, beside(shift)))

    @pl.when(y < NY - 1)
    def _():
        signal(barrier, at(y + 1, x))

    @pl.when(y > 0)
    def _():
        signal(barrier, at(y - 1, x))

    @pl.when(jnp.logical_not(is_last))
    def _():
        signal(barrier, (blk, above))

    @pl.when(is_first)
    def _():
        signal(barrier, (blk, below))

    for copy in inputs[0:2]:
        copy.wait()

    def tabulate(group, carry):
        pair = [jnp.int32(0), jnp.int32(0)]
        row = [jnp.int32(FB), jnp.int32(FB)]
        for at_pair in range(FB * KA - 1, -1, -1):
            i, k = at_pair // KA, at_pair % KA
            hit = group_ref[i, k] == group
            pair = [jnp.where(hit, at_pair, pair[0]), jnp.where(hit, pair[0], pair[1])]
            row = [jnp.where(hit, row_ref[i, k], row[0]), jnp.where(hit, row[0], row[1])]
        for slot in range(MB):
            pair_tab[MB * group + slot] = pair[slot]
            want[group % NX, pl.ds(MB * (group // NX) + slot, 1), :] = jnp.full((1, 2 * B), row[slot]).astype(F32)
        return carry

    lax.fori_loop(0, NX * NY, tabulate, 0)

    inputs[2].wait()
    tile_row = lax.broadcasted_iota(jnp.int32, (8, 2 * B), 0)
    tile_lane = lax.broadcasted_iota(jnp.int32, (8, 2 * B), 1)
    codes = jnp.zeros((8, 2 * B), F32)
    for i in range(FB):
        one = jnp.where(tile_lane < B, code_ref[0, i], code_ref[1, i]).astype(F32)
        codes = jnp.where(tile_row == i, one, codes)
    held[y, FB * B : PACK, :] = codes
    inputs[3].wait()

    pl.semaphore_wait(
        barrier,
        NX - 1 + jnp.where(y < NY - 1, 1, 0) + jnp.where(y > 0, 1, 0)
        + jnp.where(is_first, 0, 1) + jnp.where(is_last, 1, 0),
    )

    def y_copy(source, target, sender):
        slot = held.at[source]
        return pltpu.make_async_remote_copy(
            src_ref=slot, dst_ref=slot, send_sem=y_send.at[sender], recv_sem=y_recv.at[source],
            device_id=at(target, x), device_id_type=MESH,
        )

    def ask_copy(shift):
        return pltpu.make_async_remote_copy(
            src_ref=want.at[beside(shift)], dst_ref=asked.at[NX - shift],
            send_sem=ask_send.at[shift], recv_sem=ask_recv.at[NX - shift],
            device_id=at(y, beside(shift)), device_id_type=MESH,
        )

    def x_copy(source, shift):
        return pltpu.make_async_remote_copy(
            src_ref=staged.at[shift, source], dst_ref=got.at[x, source],
            send_sem=x_send.at[shift, source], recv_sem=x_recv.at[shift, source],
            device_id=at(y, beside(shift)), device_id_type=MESH,
        )

    def x_landing(source, shift):
        return pltpu.make_async_remote_copy(
            src_ref=staged.at[shift, source], dst_ref=got.at[beside(NX - shift), source],
            send_sem=x_send.at[shift, source], recv_sem=x_recv.at[shift, source],
            device_id=at(y, beside(shift)), device_id_type=MESH,
        )

    def ask_landing(shift):
        return pltpu.make_async_remote_copy(
            src_ref=want.at[beside(shift)], dst_ref=asked.at[shift],
            send_sem=ask_send.at[shift], recv_sem=ask_recv.at[shift],
            device_id=at(y, beside(shift)), device_id_type=MESH,
        )

    def halo_copy(step, side):
        return pltpu.make_async_remote_copy(
            src_ref=(down_out if side else up_out).at[step], dst_ref=(upper if side else lower).at[step],
            send_sem=halo_send.at[side, step], recv_sem=halo_recv.at[side, step],
            device_id=(blk, below if side else above), device_id_type=MESH,
        )

    order = [
        y,
        jnp.where(y == 0, 1, y - 1),
        jnp.where(y == 0, 2, jnp.where(y == 3, 1, y + 1)),
        jnp.where(y < 2, 3, 0),
    ]

    def onward(source):
        return jnp.where(source < y, y + 1, y - 1)

    def inside(target):
        return (target >= 0) & (target < NY)

    def serve(turn):
        source = order[turn]

        def choose(wanted, slot, target):
            row = wanted(MB * source + slot)
            pick = jnp.broadcast_to(row, (B, 2 * B))
            values = jnp.zeros((B, 2 * B), F32)
            code = jnp.zeros((1, 2 * B), F32)
            for i in range(FB):
                values = jnp.where(pick == i, held[source, i * B : (i + 1) * B, :], values)
                code = jnp.where(row == i, held[source, FB * B + i : FB * B + i + 1, :], code)
            target(slice(slot * B, (slot + 1) * B), values)
            target(slice(MB * B + slot, MB * B + slot + 1), code)

        for shift in (2, 1, 3):
            for slot in range(MB):

                def wanted(n, shift=shift):
                    return asked[shift, pl.ds(n, 1), :]

                def target(rows, values, shift=shift):
                    staged[shift, source, rows, :] = values

                choose(wanted, slot, target)
            x_copy(source, shift).start()
        for slot in range(MB):

            def own(n):
                return want[x, pl.ds(n, 1), :]

            def keep(rows, values):
                got[x, source, rows, :] = values

            choose(own, slot, keep)

    def y_take(turn):
        source = order[turn]
        y_copy(source, jnp.where(source < y, y - 1, y + 1), 1 + turn).wait_recv()
        target = onward(source)

        @pl.when(inside(target))
        def _():
            y_copy(source, target, 1 + turn).start()

        serve(turn)

    def x_take(turn):
        for shift in range(1, NX):
            x_landing(order[turn], shift).wait_recv()

    @pl.when(y < NY - 1)
    def _():
        y_copy(y, y + 1, 0).start()

    @pl.when(y > 0)
    def _():
        y_copy(y, y - 1, 1).start()

    for shift in (2, 1, 3):
        ask_copy(shift).start()

    @pl.when(jnp.logical_not(is_first))
    def _():
        signal(ready.at[0], (blk, below))

    @pl.when(is_last)
    def _():
        signal(ready.at[1], (blk, above))

    def windowed(values, code, at_code):
        chosen = jnp.where(code == at_code, values, 0.0)
        return chosen + pltpu.roll(chosen, B, 1)

    def left_product(i, carry):
        p_here = held[y, pl.ds(pl.multiple_of(i * B, B), B), :]
        code = jnp.broadcast_to(held[y, pl.ds(FB * B + i, 1), :], (B, 2 * B))
        parts = [windowed(p_here, code, d) for d in range(3)]
        restrict = jnp.concatenate(
            [jnp.where(first_half, parts[0], parts[1]), jnp.where(first_half, parts[2], 0.0)], axis=1
        )
        twice = []
        for side in range(2):
            both = a_ref[i, :, side * 2 * B : (side + 1) * 2 * B]
            turned = pltpu.roll(both, B, 1)
            twice += [jnp.where(first_half, both, turned), jnp.where(first_half, turned, both)]
        result = lax.dot_general(
            restrict, jnp.concatenate(twice, axis=1), (((0,), (0,)), ((), ())),
            precision=lax.Precision.HIGHEST, preferred_element_type=F32,
        )[0 : 3 * B]
        high = result.astype(BF16)
        low = (result - high.astype(F32)).astype(BF16)
        for k in range(KA):
            left_hi[i * KA + k] = high[:, k * 2 * B : (k + 1) * 2 * B]
            left_lo[i * KA + k] = low[:, k * 2 * B : (k + 1) * 2 * B]
        return carry

    wide_half = lax.broadcasted_iota(jnp.int32, (3 * B, 2 * B), 1) < B

    def compute(step):
        for half in range(2):
            row, column = step // 2, 2 * (step % 2) + half
            for slot in range(MB):
                values = got[column, row, slot * B : (slot + 1) * B, :]
                code = jnp.broadcast_to(got[column, row, MB * B + slot : MB * B + slot + 1, :], (B, 2 * B))
                mine = first_half if half == 0 else jnp.logical_not(first_half)
                at_row = (MB * half + slot) * B
                for e in range(3):
                    part = jnp.where(mine, windowed(values, code, e), 0.0)
                    high = part.astype(BF16)
                    win_hi[at_row : at_row + B, e * 2 * B : (e + 1) * 2 * B] = high
                    win_lo[at_row : at_row + B, e * 2 * B : (e + 1) * 2 * B] = (part - high.astype(F32)).astype(BF16)

        def stacked(ref):
            pairs = [ref[pair_tab[2 * MB * step + n]] for n in range(2 * MB)]
            return jnp.concatenate(
                [jnp.where(wide_half, pairs[0], pairs[1]), jnp.where(wide_half, pairs[2], pairs[3])], axis=1
            )

        high, low = stacked(left_hi), stacked(left_lo)
        total = jnp.dot(high, win_hi[...], preferred_element_type=F32)
        total += jnp.dot(high, win_lo[...], preferred_element_type=F32)
        total += jnp.dot(low, win_hi[...], preferred_element_type=F32)
        down_out[step] = total[0:B]
        middle[step] = total[B : 2 * B]
        up_out[step] = total[2 * B : 3 * B]

    def send_up(step):
        halo_copy(step, 0).start()

    def send_down(step):
        halo_copy(step, 1).start()

    def finish(step):
        halo_copy(step, 0).wait_recv()
        halo_copy(step, 1).wait_recv()
        for e in range(5):
            parts = []
            for ref, shift in ((lower, 0), (middle, 1), (upper, 2)):
                if 0 <= e - shift < 3:
                    parts.append(ref[step, :, (e - shift) * 2 * B : (e - shift + 1) * 2 * B])
            column = pl.multiple_of(e * NX * NY * B + step * 2 * B, 2 * B)
            out_ref[:, pl.ds(column, 2 * B)] = sum(parts[1:], parts[0])

    def both_steps(turn, *work):
        def one(n, carry):
            for each in work:
                each(2 * order[turn] + n)
            return carry

        lax.fori_loop(0, 2, one, 0)

    inputs[4].wait()
    lax.fori_loop(0, 2, left_product, 0)
    for shift in range(1, NX):
        ask_landing(shift).wait_recv()
    serve(0)
    lax.fori_loop(2, 3, left_product, 0)
    y_take(1)
    lax.fori_loop(3, 4, left_product, 0)
    y_take(2)
    x_take(0)

    @pl.when(jnp.logical_not(is_last))
    def _():
        pl.semaphore_wait(ready.at[0], 1)

    both_steps(0, compute, send_up)

    @pl.when(jnp.logical_not(is_first))
    def _():
        both_steps(0, send_down)

    y_take(3)
    x_take(1)
    both_steps(1, compute, send_up)

    @pl.when(is_first)
    def _():
        pl.semaphore_wait(ready.at[1], 1)
        both_steps(0, send_down)

    both_steps(1, send_down)
    x_take(2)
    both_steps(2, compute, send_up, send_down)
    x_take(3)
    both_steps(3, compute, send_up, send_down)
    for turn in range(4):
        both_steps(turn, finish)

    @pl.when(y < NY - 1)
    def _():
        y_copy(y, y + 1, 0).wait_send()

    @pl.when(y > 0)
    def _():
        y_copy(y, y - 1, 1).wait_send()

    for turn in range(1, 4):
        target = onward(order[turn])

        @pl.when(inside(target))
        def _():
            y_copy(order[turn], target, 1 + turn).wait_send()

    for shift in range(1, NX):
        ask_copy(shift).wait_send()

    def drain_x(source, carry):
        for shift in range(1, NX):
            x_copy(source, shift).wait_send()
        return carry

    lax.fori_loop(0, NY, drain_x, 0)

    def drain_halo(step, carry):
        halo_copy(step, 0).wait_send()
        halo_copy(step, 1).wait_send()
        return carry

    lax.fori_loop(0, STEPS, drain_halo, 0)


def body(fine_blocks, source_group, source_row, prolong_blocks, prolong_code):
    hbm = pl.BlockSpec(memory_space=pltpu.HBM)
    window = 3 * 2 * B
    halo = pltpu.VMEM((STEPS, B, window), F32)
    dma = pltpu.SemaphoreType.DMA
    return pl.pallas_call(
        kernel,
        out_shape=jax.ShapeDtypeStruct((B, 5 * NX * NY * B), F32),
        in_specs=[hbm] * 5,
        out_specs=pl.BlockSpec(memory_space=pltpu.VMEM),
        scratch_shapes=[
            pltpu.VMEM((FB, B, KA * B), F32),
            pltpu.SMEM((FB, KA), jnp.int32),
            pltpu.SMEM((FB, KA), jnp.int32),
            pltpu.SMEM((2, FB), jnp.int32),
            pltpu.VMEM((NY, PACK, 2 * B), F32),
            pltpu.VMEM((NX, NY * MB, 2 * B), F32),
            pltpu.VMEM((NX, NY * MB, 2 * B), F32),
            pltpu.VMEM((NX, NY, SHARE, 2 * B), F32),
            pltpu.VMEM((NX, NY, SHARE, 2 * B), F32),
            pltpu.VMEM((FB * KA, 3 * B, 2 * B), BF16),
            pltpu.VMEM((FB * KA, 3 * B, 2 * B), BF16),
            pltpu.VMEM((2 * MB * B, window), BF16),
            pltpu.VMEM((2 * MB * B, window), BF16),
            halo, halo, halo, halo, halo,
            pltpu.SMEM((MB * NX * NY,), jnp.int32),
            dma((5,)),
            dma((5,)), dma((NY,)),
            dma((NX,)), dma((NX,)),
            dma((NX, NY)), dma((NX, NY)),
            dma((2, STEPS)), dma((2, STEPS)),
            pltpu.SemaphoreType.REGULAR((2,)),
        ],
        compiler_params=pltpu.CompilerParams(
            collective_id=0, has_side_effects=True, vmem_limit_bytes=60 * 2**20
        ),
        cost_estimate=pl.CostEstimate(flops=10**9, bytes_accessed=4 * 2**20, transcendentals=0),
        name="galerkin",
    )(fine_blocks, prolong_blocks.reshape(FB * B, 2 * B), source_group, source_row, prolong_code.T)


def solution(mesh):
    return jax.shard_map(
        body,
        mesh=mesh,
        in_specs=(
            P(("blk", "band"), None, None),
            P(("blk", "band"), None),
            P(("blk", "band"), None),
            P(("blk", "band"), None, None),
            P(("blk", "band"), None),
        ),
        out_specs=P(("blk", "band"), None),
        check_vma=False,
    )
```

```python
import jax
import jax.numpy as jnp
from jax import lax
from jax.experimental import pallas as pl
from jax.experimental.pallas import tpu as pltpu
from jax.sharding import PartitionSpec as P

MESH = pl.DeviceIdType.MESH
F32 = jnp.float32
BF16 = jnp.bfloat16

B = 64
FB = 4
KA = 4
MB = 2
NX = 4
NY = 4
PACK = FB * B + 8
SHARE = MB * B + 8
STEPS = NX * NY // 2
DETOURS = 4


def kernel(
    a_hbm, p_hbm, group_hbm, row_hbm, code_hbm, out_ref,
    a_ref, group_ref, row_ref, code_ref,
    held, want, asked, staged, got, left_hi, left_lo, win_hi, win_lo,
    middle, up_out, down_out, lower, upper, passing, pair_tab,
    in_sem, y_send, y_recv, ask_send, ask_recv, x_send, x_recv, halo_send, halo_recv,
    pass_send, pass_recv, on_send, ready,
):
    blk, band = lax.axis_index("blk"), lax.axis_index("band")
    bands = lax.axis_size("band")
    half_bands = bands // 2
    y, x = blk // NX, blk % NX
    above, below = (band + 1) % bands, (band + bands - 1) % bands
    place = band % half_bands
    is_first, is_last = place == 0, place == half_bands - 1
    far = half_bands >= 4
    is_patient, is_passer = place == half_bands - 2, place == half_bands - 3
    lane = lax.broadcasted_iota(jnp.int32, (B, 2 * B), 1)
    first_half = lane < B

    def at(row, column):
        return (row * NX + column, band)

    def beside(shift):
        return (x + shift) % NX

    def signal(semaphore, target):
        pl.semaphore_signal(semaphore, inc=1, device_id=target, device_id_type=MESH)

    inputs = [
        pltpu.make_async_copy(source, target, in_sem.at[n])
        for n, (source, target) in enumerate((
            (group_hbm, group_ref), (row_hbm, row_ref), (code_hbm, code_ref),
            (p_hbm, held.at[y, pl.ds(0, FB * B)]), (a_hbm, a_ref),
        ))
    ]
    for copy in inputs:
        copy.start()

    barrier = pltpu.get_barrier_semaphore()
    for shift in range(1, NX):
        signal(barrier, at(y, beside(shift)))

    @pl.when(y < NY - 1)
    def _():
        signal(barrier, at(y + 1, x))

    @pl.when(y > 0)
    def _():
        signal(barrier, at(y - 1, x))

    @pl.when(jnp.logical_not(is_last))
    def _():
        signal(barrier, (blk, above))

    @pl.when(is_first)
    def _():
        signal(barrier, (blk, below))
        if far:
            signal(barrier, (blk, (band + bands - 3) % bands))

    if far:

        @pl.when(is_passer)
        def _():
            signal(barrier, (blk, band + 2))

    for copy in inputs[0:2]:
        copy.wait()

    def tabulate(group, carry):
        pair = [jnp.int32(0), jnp.int32(0)]
        row = [jnp.int32(FB), jnp.int32(FB)]
        for at_pair in range(FB * KA - 1, -1, -1):
            i, k = at_pair // KA, at_pair % KA
            hit = group_ref[i, k] == group
            pair = [jnp.where(hit, at_pair, pair[0]), jnp.where(hit, pair[0], pair[1])]
            row = [jnp.where(hit, row_ref[i, k], row[0]), jnp.where(hit, row[0], row[1])]
        for slot in range(MB):
            pair_tab[MB * group + slot] = pair[slot]
            want[group % NX, pl.ds(MB * (group // NX) + slot, 1), :] = jnp.full((1, 2 * B), row[slot]).astype(F32)
        return carry

    lax.fori_loop(0, NX * NY, tabulate, 0)

    inputs[2].wait()
    tile_row = lax.broadcasted_iota(jnp.int32, (8, 2 * B), 0)
    tile_lane = lax.broadcasted_iota(jnp.int32, (8, 2 * B), 1)
    codes = jnp.zeros((8, 2 * B), F32)
    for i in range(FB):
        one = jnp.where(tile_lane < B, code_ref[0, i], code_ref[1, i]).astype(F32)
        codes = jnp.where(tile_row == i, one, codes)
    held[y, FB * B : PACK, :] = codes
    inputs[3].wait()

    pl.semaphore_wait(
        barrier,
        NX - 1 + jnp.where(y < NY - 1, 1, 0) + jnp.where(y > 0, 1, 0)
        + jnp.where(is_first, 0, 1) + jnp.where(is_last, 2 if far else 1, 0)
        + (jnp.where(is_passer, 1, 0) if far else 0),
    )

    def y_copy(source, target, sender):
        slot = held.at[source]
        return pltpu.make_async_remote_copy(
            src_ref=slot, dst_ref=slot, send_sem=y_send.at[sender], recv_sem=y_recv.at[source],
            device_id=at(target, x), device_id_type=MESH,
        )

    def ask_copy(shift):
        return pltpu.make_async_remote_copy(
            src_ref=want.at[beside(shift)], dst_ref=asked.at[NX - shift],
            send_sem=ask_send.at[shift], recv_sem=ask_recv.at[NX - shift],
            device_id=at(y, beside(shift)), device_id_type=MESH,
        )

    def x_copy(source, shift):
        return pltpu.make_async_remote_copy(
            src_ref=staged.at[shift, source], dst_ref=got.at[x, source],
            send_sem=x_send.at[shift, source], recv_sem=x_recv.at[shift, source],
            device_id=at(y, beside(shift)), device_id_type=MESH,
        )

    def x_landing(source, shift):
        return pltpu.make_async_remote_copy(
            src_ref=staged.at[shift, source], dst_ref=got.at[beside(NX - shift), source],
            send_sem=x_send.at[shift, source], recv_sem=x_recv.at[shift, source],
            device_id=at(y, beside(shift)), device_id_type=MESH,
        )

    def ask_landing(shift):
        return pltpu.make_async_remote_copy(
            src_ref=want.at[beside(shift)], dst_ref=asked.at[shift],
            send_sem=ask_send.at[shift], recv_sem=ask_recv.at[shift],
            device_id=at(y, beside(shift)), device_id_type=MESH,
        )

    def halo_copy(step, side):
        return pltpu.make_async_remote_copy(
            src_ref=(down_out if side else up_out).at[step], dst_ref=(upper if side else lower).at[step],
            send_sem=halo_send.at[side, step], recv_sem=halo_recv.at[side, step],
            device_id=(blk, below if side else above), device_id_type=MESH,
        )

    def pass_copy(step, n):
        return pltpu.make_async_remote_copy(
            src_ref=up_out.at[step], dst_ref=passing.at[n], send_sem=pass_send.at[n], recv_sem=pass_recv.at[n],
            device_id=(blk, (band + bands - 2) % bands), device_id_type=MESH,
        )

    def on_copy(step, n):
        return pltpu.make_async_remote_copy(
            src_ref=passing.at[n], dst_ref=lower.at[step], send_sem=on_send.at[n], recv_sem=halo_recv.at[0, step],
            device_id=(blk, (band + 3) % bands), device_id_type=MESH,
        )

    order = [
        y,
        jnp.where(y == 0, 1, y - 1),
        jnp.where(y == 0, 2, jnp.where(y == 3, 1, y + 1)),
        jnp.where(y < 2, 3, 0),
    ]

    def onward(source):
        return jnp.where(source < y, y + 1, y - 1)

    def inside(target):
        return (target >= 0) & (target < NY)

    def serve(turn):
        source = order[turn]

        def choose(wanted, slot, target):
            row = wanted(MB * source + slot)
            pick = jnp.broadcast_to(row, (B, 2 * B))
            values = jnp.zeros((B, 2 * B), F32)
            code = jnp.zeros((1, 2 * B), F32)
            for i in range(FB):
                values = jnp.where(pick == i, held[source, i * B : (i + 1) * B, :], values)
                code = jnp.where(row == i, held[source, FB * B + i : FB * B + i + 1, :], code)
            target(slice(slot * B, (slot + 1) * B), values)
            target(slice(MB * B + slot, MB * B + slot + 1), code)

        for shift in (2, 1, 3):
            for slot in range(MB):

                def wanted(n, shift=shift):
                    return asked[shift, pl.ds(n, 1), :]

                def target(rows, values, shift=shift):
                    staged[shift, source, rows, :] = values

                choose(wanted, slot, target)
            x_copy(source, shift).start()
        for slot in range(MB):

            def own(n):
                return want[x, pl.ds(n, 1), :]

            def keep(rows, values):
                got[x, source, rows, :] = values

            choose(own, slot, keep)

    def y_take(turn):
        source = order[turn]
        y_copy(source, jnp.where(source < y, y - 1, y + 1), 1 + turn).wait_recv()
        target = onward(source)

        @pl.when(inside(target))
        def _():
            y_copy(source, target, 1 + turn).start()

        serve(turn)

    def x_take(turn):
        for shift in range(1, NX):
            x_landing(order[turn], shift).wait_recv()

    @pl.when(jnp.logical_not(is_first))
    def _():
        signal(ready.at[0], (blk, below))

    @pl.when(is_last)
    def _():
        signal(ready.at[1], (blk, above))

    if far:

        @pl.when(is_patient)
        def _():
            pl.semaphore_wait(ready.at[2], 1)

    @pl.when(y < NY - 1)
    def _():
        y_copy(y, y + 1, 0).start()

    @pl.when(y > 0)
    def _():
        y_copy(y, y - 1, 1).start()

    for shift in (2, 1, 3):
        ask_copy(shift).start()

    def windowed(values, code, at_code):
        chosen = jnp.where(code == at_code, values, 0.0)
        return chosen + pltpu.roll(chosen, B, 1)

    def left_product(i, carry):
        p_here = held[y, pl.ds(pl.multiple_of(i * B, B), B), :]
        code = jnp.broadcast_to(held[y, pl.ds(FB * B + i, 1), :], (B, 2 * B))
        parts = [windowed(p_here, code, d) for d in range(3)]
        restrict = jnp.concatenate(
            [jnp.where(first_half, parts[0], parts[1]), jnp.where(first_half, parts[2], 0.0)], axis=1
        )
        twice = []
        for side in range(2):
            both = a_ref[i, :, side * 2 * B : (side + 1) * 2 * B]
            turned = pltpu.roll(both, B, 1)
            twice += [jnp.where(first_half, both, turned), jnp.where(first_half, turned, both)]
        result = lax.dot_general(
            restrict, jnp.concatenate(twice, axis=1), (((0,), (0,)), ((), ())),
            precision=lax.Precision.HIGHEST, preferred_element_type=F32,
        )[0 : 3 * B]
        high = result.astype(BF16)
        low = (result - high.astype(F32)).astype(BF16)
        for k in range(KA):
            left_hi[i * KA + k] = high[:, k * 2 * B : (k + 1) * 2 * B]
            left_lo[i * KA + k] = low[:, k * 2 * B : (k + 1) * 2 * B]
        return carry

    wide_half = lax.broadcasted_iota(jnp.int32, (3 * B, 2 * B), 1) < B

    def compute(step):
        for half in range(2):
            row, column = step // 2, 2 * (step % 2) + half
            for slot in range(MB):
                values = got[column, row, slot * B : (slot + 1) * B, :]
                code = jnp.broadcast_to(got[column, row, MB * B + slot : MB * B + slot + 1, :], (B, 2 * B))
                mine = first_half if half == 0 else jnp.logical_not(first_half)
                at_row = (MB * half + slot) * B
                for e in range(3):
                    part = jnp.where(mine, windowed(values, code, e), 0.0)
                    high = part.astype(BF16)
                    win_hi[at_row : at_row + B, e * 2 * B : (e + 1) * 2 * B] = high
                    win_lo[at_row : at_row + B, e * 2 * B : (e + 1) * 2 * B] = (part - high.astype(F32)).astype(BF16)

        def stacked(ref):
            pairs = [ref[pair_tab[2 * MB * step + n]] for n in range(2 * MB)]
            return jnp.concatenate(
                [jnp.where(wide_half, pairs[0], pairs[1]), jnp.where(wide_half, pairs[2], pairs[3])], axis=1
            )

        high, low = stacked(left_hi), stacked(left_lo)
        total = jnp.dot(high, win_hi[...], preferred_element_type=F32)
        total += jnp.dot(high, win_lo[...], preferred_element_type=F32)
        total += jnp.dot(low, win_hi[...], preferred_element_type=F32)
        down_out[step] = total[0:B]
        middle[step] = total[B : 2 * B]
        up_out[step] = total[2 * B : 3 * B]

    def send_up(turn):
        def start(n, direct):
            step = 2 * order[turn] + n
            if direct:
                halo_copy(step, 0).start()
            else:
                pass_copy(step, 2 * turn + n).start()

        up_either(turn, start)

    def up_either(turn, act):
        if far and 2 * turn < DETOURS:

            @pl.when(is_last)
            def _():
                act(0, False)
                act(1, False)

            @pl.when(jnp.logical_not(is_last))
            def _():
                act(0, True)
                act(1, True)
        else:
            act(0, True)
            act(1, True)

    def pass_on(turn):
        if far:

            @pl.when(is_passer)
            def _():
                for n in range(2):
                    step = 2 * order[turn] + n
                    pass_copy(step, 2 * turn + n).wait_recv()
                    on_copy(step, 2 * turn + n).start()

    def send_down(step):
        halo_copy(step, 1).start()

    def finish(step):
        halo_copy(step, 0).wait_recv()
        halo_copy(step, 1).wait_recv()
        for e in range(5):
            parts = []
            for ref, shift in ((lower, 0), (middle, 1), (upper, 2)):
                if 0 <= e - shift < 3:
                    parts.append(ref[step, :, (e - shift) * 2 * B : (e - shift + 1) * 2 * B])
            column = pl.multiple_of(e * NX * NY * B + step * 2 * B, 2 * B)
            out_ref[:, pl.ds(column, 2 * B)] = sum(parts[1:], parts[0])

    def both_steps(turn, *work):
        def one(n, carry):
            for each in work:
                each(2 * order[turn] + n)
            return carry

        lax.fori_loop(0, 2, one, 0)

    inputs[4].wait()
    lax.fori_loop(0, 2, left_product, 0)
    for shift in range(1, NX):
        ask_landing(shift).wait_recv()
    serve(0)
    lax.fori_loop(2, 3, left_product, 0)
    y_take(1)
    lax.fori_loop(3, 4, left_product, 0)
    y_take(2)
    x_take(0)

    @pl.when(jnp.logical_not(is_last))
    def _():
        pl.semaphore_wait(ready.at[0], 1)

    both_steps(0, compute)
    send_up(0)

    @pl.when(jnp.logical_not(is_first))
    def _():
        both_steps(0, send_down)

    y_take(3)
    x_take(1)
    both_steps(1, compute)
    send_up(1)

    @pl.when(is_first)
    def _():
        pl.semaphore_wait(ready.at[1], 1)
        both_steps(0, send_down)

    both_steps(1, send_down)
    pass_on(0)
    x_take(2)
    both_steps(2, compute)
    send_up(2)
    both_steps(2, send_down)
    pass_on(1)
    x_take(3)
    if far:

        @pl.when(is_last)
        def _():
            signal(ready.at[2], (blk, below))

    both_steps(3, compute)
    send_up(3)
    both_steps(3, send_down)
    for turn in range(4):
        both_steps(turn, finish)

    @pl.when(y < NY - 1)
    def _():
        y_copy(y, y + 1, 0).wait_send()

    @pl.when(y > 0)
    def _():
        y_copy(y, y - 1, 1).wait_send()

    for turn in range(1, 4):
        target = onward(order[turn])

        @pl.when(inside(target))
        def _():
            y_copy(order[turn], target, 1 + turn).wait_send()

    for shift in range(1, NX):
        ask_copy(shift).wait_send()

    def drain_x(source, carry):
        for shift in range(1, NX):
            x_copy(source, shift).wait_send()
        return carry

    lax.fori_loop(0, NY, drain_x, 0)

    def drain_halo(step, carry):
        halo_copy(step, 1).wait_send()
        return carry

    lax.fori_loop(0, STEPS, drain_halo, 0)
    for turn in range(4):

        def drain_up(n, direct, turn=turn):
            step = 2 * order[turn] + n
            if direct:
                halo_copy(step, 0).wait_send()
            else:
                pass_copy(step, 2 * turn + n).wait_send()

        up_either(turn, drain_up)
    if far:

        @pl.when(is_passer)
        def _():
            for n in range(DETOURS):
                on_copy(2 * order[n // 2] + n % 2, n).wait_send()


def body(fine_blocks, source_group, source_row, prolong_blocks, prolong_code):
    hbm = pl.BlockSpec(memory_space=pltpu.HBM)
    window = 3 * 2 * B
    halo = pltpu.VMEM((STEPS, B, window), F32)
    dma = pltpu.SemaphoreType.DMA
    return pl.pallas_call(
        kernel,
        out_shape=jax.ShapeDtypeStruct((B, 5 * NX * NY * B), F32),
        in_specs=[hbm] * 5,
        out_specs=pl.BlockSpec(memory_space=pltpu.VMEM),
        scratch_shapes=[
            pltpu.VMEM((FB, B, KA * B), F32),
            pltpu.SMEM((FB, KA), jnp.int32),
            pltpu.SMEM((FB, KA), jnp.int32),
            pltpu.SMEM((2, FB), jnp.int32),
            pltpu.VMEM((NY, PACK, 2 * B), F32),
            pltpu.VMEM((NX, NY * MB, 2 * B), F32),
            pltpu.VMEM((NX, NY * MB, 2 * B), F32),
            pltpu.VMEM((NX, NY, SHARE, 2 * B), F32),
            pltpu.VMEM((NX, NY, SHARE, 2 * B), F32),
            pltpu.VMEM((FB * KA, 3 * B, 2 * B), BF16),
            pltpu.VMEM((FB * KA, 3 * B, 2 * B), BF16),
            pltpu.VMEM((2 * MB * B, window), BF16),
            pltpu.VMEM((2 * MB * B, window), BF16),
            halo, halo, halo, halo, halo,
            pltpu.VMEM((DETOURS, B, window), F32),
            pltpu.SMEM((MB * NX * NY,), jnp.int32),
            dma((5,)),
            dma((5,)), dma((NY,)),
            dma((NX,)), dma((NX,)),
            dma((NX, NY)), dma((NX, NY)),
            dma((2, STEPS)), dma((2, STEPS)),
            dma((DETOURS,)), dma((DETOURS,)), dma((DETOURS,)),
            pltpu.SemaphoreType.REGULAR((3,)),
        ],
        compiler_params=pltpu.CompilerParams(
            collective_id=0, has_side_effects=True, vmem_limit_bytes=60 * 2**20
        ),
        cost_estimate=pl.CostEstimate(flops=10**9, bytes_accessed=4 * 2**20, transcendentals=0),
        name="galerkin",
    )(fine_blocks, prolong_blocks.reshape(FB * B, 2 * B), source_group, source_row, prolong_code.T)


def solution(mesh):
    return jax.shard_map(
        body,
        mesh=mesh,
        in_specs=(
            P(("blk", "band"), None, None),
            P(("blk", "band"), None),
            P(("blk", "band"), None),
            P(("blk", "band"), None, None),
            P(("blk", "band"), None),
        ),
        out_specs=P(("blk", "band"), None),
        check_vma=False,
    )
```

```python
import jax
import jax.numpy as jnp
from jax import lax
from jax.experimental import pallas as pl
from jax.experimental.pallas import tpu as pltpu
from jax.sharding import PartitionSpec as P

MESH = pl.DeviceIdType.MESH
F32 = jnp.float32
BF16 = jnp.bfloat16

B = 64
FB = 4
KA = 4
MB = 2
NX = 4
NY = 4
PACK = FB * B + 8
SHARE = MB * B + 8
STEPS = NX * NY // 2
DETOURS = 4


def kernel(
    a_hbm, p_hbm, group_hbm, row_hbm, code_hbm, out_ref,
    a_ref, group_ref, row_ref, code_ref,
    held, want, asked, staged, got, left_hi, left_lo, win_hi, win_lo,
    middle, up_out, down_out, lower, upper, passing, pair_tab,
    in_sem, y_send, y_recv, ask_send, ask_recv, x_send, x_recv, halo_send, halo_recv,
    pass_send, pass_recv, on_send, ready,
):
    blk, band = lax.axis_index("blk"), lax.axis_index("band")
    bands = lax.axis_size("band")
    half_bands = bands // 2
    y, x = blk // NX, blk % NX
    above, below = (band + 1) % bands, (band + bands - 1) % bands
    place = band % half_bands
    is_first, is_last = place == 0, place == half_bands - 1
    far = half_bands >= 4
    is_patient, is_passer = place == half_bands - 2, place == half_bands - 3
    lane = lax.broadcasted_iota(jnp.int32, (B, 2 * B), 1)
    first_half = lane < B

    def at(row, column):
        return (row * NX + column, band)

    def inside(row):
        return (row >= 0) & (row < NY)

    def beside(shift):
        return (x + shift) % NX

    def signal(semaphore, target):
        pl.semaphore_signal(semaphore, inc=1, device_id=target, device_id_type=MESH)

    inputs = [
        pltpu.make_async_copy(source, target, in_sem.at[n])
        for n, (source, target) in enumerate((
            (group_hbm, group_ref), (row_hbm, row_ref), (code_hbm, code_ref),
            (p_hbm, held.at[y, pl.ds(0, FB * B)]), (a_hbm, a_ref),
        ))
    ]
    for copy in inputs:
        copy.start()

    barrier = pltpu.get_barrier_semaphore()
    for shift in range(1, NX):
        signal(barrier, at(y, beside(shift)))

    for jump in (1, -1, 2, -2):

        @pl.when(inside(y + jump))
        def _():
            signal(barrier, at(y + jump, x))

    @pl.when(jnp.logical_not(is_last))
    def _():
        signal(barrier, (blk, above))

    @pl.when(is_first)
    def _():
        signal(barrier, (blk, below))
        if far:
            signal(barrier, (blk, (band + bands - 3) % bands))

    if far:

        @pl.when(is_passer)
        def _():
            signal(barrier, (blk, band + 2))

    for copy in inputs[0:2]:
        copy.wait()

    def tabulate(group, carry):
        pair = [jnp.int32(0), jnp.int32(0)]
        row = [jnp.int32(FB), jnp.int32(FB)]
        for at_pair in range(FB * KA - 1, -1, -1):
            i, k = at_pair // KA, at_pair % KA
            hit = group_ref[i, k] == group
            pair = [jnp.where(hit, at_pair, pair[0]), jnp.where(hit, pair[0], pair[1])]
            row = [jnp.where(hit, row_ref[i, k], row[0]), jnp.where(hit, row[0], row[1])]
        for slot in range(MB):
            pair_tab[MB * group + slot] = pair[slot]
            want[group % NX, pl.ds(MB * (group // NX) + slot, 1), :] = jnp.full((1, 2 * B), row[slot]).astype(F32)
        return carry

    lax.fori_loop(0, NX * NY, tabulate, 0)

    inputs[2].wait()
    tile_row = lax.broadcasted_iota(jnp.int32, (8, 2 * B), 0)
    tile_lane = lax.broadcasted_iota(jnp.int32, (8, 2 * B), 1)
    codes = jnp.zeros((8, 2 * B), F32)
    for i in range(FB):
        one = jnp.where(tile_lane < B, code_ref[0, i], code_ref[1, i]).astype(F32)
        codes = jnp.where(tile_row == i, one, codes)
    held[y, FB * B : PACK, :] = codes
    inputs[3].wait()

    pl.semaphore_wait(
        barrier,
        NX - 1 + sum(jnp.where(inside(y + jump), 1, 0) for jump in (1, -1, 2, -2))
        + jnp.where(is_first, 0, 1) + jnp.where(is_last, 2 if far else 1, 0)
        + (jnp.where(is_passer, 1, 0) if far else 0),
    )

    def y_copy(source, target, sender):
        slot = held.at[source]
        return pltpu.make_async_remote_copy(
            src_ref=slot, dst_ref=slot, send_sem=y_send.at[sender], recv_sem=y_recv.at[source],
            device_id=at(target, x), device_id_type=MESH,
        )

    def ask_copy(shift):
        return pltpu.make_async_remote_copy(
            src_ref=want.at[beside(shift)], dst_ref=asked.at[NX - shift],
            send_sem=ask_send.at[shift], recv_sem=ask_recv.at[NX - shift],
            device_id=at(y, beside(shift)), device_id_type=MESH,
        )

    def x_copy(source, shift):
        return pltpu.make_async_remote_copy(
            src_ref=staged.at[shift, source], dst_ref=got.at[x, source],
            send_sem=x_send.at[shift, source], recv_sem=x_recv.at[shift, source],
            device_id=at(y, beside(shift)), device_id_type=MESH,
        )

    def x_landing(source, shift):
        return pltpu.make_async_remote_copy(
            src_ref=staged.at[shift, source], dst_ref=got.at[beside(NX - shift), source],
            send_sem=x_send.at[shift, source], recv_sem=x_recv.at[shift, source],
            device_id=at(y, beside(shift)), device_id_type=MESH,
        )

    def ask_landing(shift):
        return pltpu.make_async_remote_copy(
            src_ref=want.at[beside(shift)], dst_ref=asked.at[shift],
            send_sem=ask_send.at[shift], recv_sem=ask_recv.at[shift],
            device_id=at(y, beside(shift)), device_id_type=MESH,
        )

    def halo_copy(step, side):
        return pltpu.make_async_remote_copy(
            src_ref=(down_out if side else up_out).at[step], dst_ref=(upper if side else lower).at[step],
            send_sem=halo_send.at[side, step], recv_sem=halo_recv.at[side, step],
            device_id=(blk, below if side else above), device_id_type=MESH,
        )

    def pass_copy(step, n):
        return pltpu.make_async_remote_copy(
            src_ref=up_out.at[step], dst_ref=passing.at[n], send_sem=pass_send.at[n], recv_sem=pass_recv.at[n],
            device_id=(blk, (band + bands - 2) % bands), device_id_type=MESH,
        )

    def on_copy(step, n):
        return pltpu.make_async_remote_copy(
            src_ref=passing.at[n], dst_ref=lower.at[step], send_sem=on_send.at[n], recv_sem=halo_recv.at[0, step],
            device_id=(blk, (band + 3) % bands), device_id_type=MESH,
        )

    order = [
        y,
        jnp.where(y == 0, 1, y - 1),
        jnp.where(y == 0, 2, jnp.where(y == 3, 1, y + 1)),
        jnp.where(y < 2, 3, 0),
    ]

    def hands_on(source):
        return ((y == 2) & (source == 0)) | ((y == 1) & (source == 3))

    hand_target = jnp.where(y == 2, 3, 0)
    is_end = (y == 0) | (y == NY - 1)

    def serve(turn):
        source = order[turn]

        def choose(wanted, slot, target):
            row = wanted(MB * source + slot)
            pick = jnp.broadcast_to(row, (B, 2 * B))
            values = jnp.zeros((B, 2 * B), F32)
            code = jnp.zeros((1, 2 * B), F32)
            for i in range(FB):
                values = jnp.where(pick == i, held[source, i * B : (i + 1) * B, :], values)
                code = jnp.where(row == i, held[source, FB * B + i : FB * B + i + 1, :], code)
            target(slice(slot * B, (slot + 1) * B), values)
            target(slice(MB * B + slot, MB * B + slot + 1), code)

        for shift in (2, 1, 3):
            for slot in range(MB):

                def wanted(n, shift=shift):
                    return asked[shift, pl.ds(n, 1), :]

                def target(rows, values, shift=shift):
                    staged[shift, source, rows, :] = values

                choose(wanted, slot, target)
            x_copy(source, shift).start()
        for slot in range(MB):

            def own(n):
                return want[x, pl.ds(n, 1), :]

            def keep(rows, values):
                got[x, source, rows, :] = values

            choose(own, slot, keep)

    def y_take(turn):
        source = order[turn]
        y_copy(source, jnp.where(source < y, y - 1, y + 1), 0).wait_recv()

        @pl.when(hands_on(source))
        def _():
            y_copy(source, hand_target, 4).start()

    def x_take(turn):
        for shift in range(1, NX):
            x_landing(order[turn], shift).wait_recv()

    @pl.when(jnp.logical_not(is_first))
    def _():
        signal(ready.at[0], (blk, below))

    @pl.when(is_last)
    def _():
        signal(ready.at[1], (blk, above))

    for n, jump in enumerate((1, -1, 2, -2)):

        @pl.when(inside(y + jump))
        def _():
            y_copy(y, y + jump, n).start()

    for shift in (2, 1, 3):
        ask_copy(shift).start()

    def windowed(values, code, at_code):
        chosen = jnp.where(code == at_code, values, 0.0)
        return chosen + pltpu.roll(chosen, B, 1)

    def left_product(i, carry):
        p_here = held[y, pl.ds(pl.multiple_of(i * B, B), B), :]
        code = jnp.broadcast_to(held[y, pl.ds(FB * B + i, 1), :], (B, 2 * B))
        parts = [windowed(p_here, code, d) for d in range(3)]
        restrict = jnp.concatenate(
            [jnp.where(first_half, parts[0], parts[1]), jnp.where(first_half, parts[2], 0.0)], axis=1
        )
        twice = []
        for side in range(2):
            both = a_ref[i, :, side * 2 * B : (side + 1) * 2 * B]
            turned = pltpu.roll(both, B, 1)
            twice += [jnp.where(first_half, both, turned), jnp.where(first_half, turned, both)]
        result = lax.dot_general(
            restrict, jnp.concatenate(twice, axis=1), (((0,), (0,)), ((), ())),
            precision=lax.Precision.HIGHEST, preferred_element_type=F32,
        )[0 : 3 * B]
        high = result.astype(BF16)
        low = (result - high.astype(F32)).astype(BF16)
        for k in range(KA):
            left_hi[i * KA + k] = high[:, k * 2 * B : (k + 1) * 2 * B]
            left_lo[i * KA + k] = low[:, k * 2 * B : (k + 1) * 2 * B]
        return carry

    wide_half = lax.broadcasted_iota(jnp.int32, (3 * B, 2 * B), 1) < B

    def compute(step):
        for half in range(2):
            row, column = step // 2, 2 * (step % 2) + half
            for slot in range(MB):
                values = got[column, row, slot * B : (slot + 1) * B, :]
                code = jnp.broadcast_to(got[column, row, MB * B + slot : MB * B + slot + 1, :], (B, 2 * B))
                mine = first_half if half == 0 else jnp.logical_not(first_half)
                at_row = (MB * half + slot) * B
                for e in range(3):
                    part = jnp.where(mine, windowed(values, code, e), 0.0)
                    high = part.astype(BF16)
                    win_hi[at_row : at_row + B, e * 2 * B : (e + 1) * 2 * B] = high
                    win_lo[at_row : at_row + B, e * 2 * B : (e + 1) * 2 * B] = (part - high.astype(F32)).astype(BF16)

        def stacked(ref):
            pairs = [ref[pair_tab[2 * MB * step + n]] for n in range(2 * MB)]
            return jnp.concatenate(
                [jnp.where(wide_half, pairs[0], pairs[1]), jnp.where(wide_half, pairs[2], pairs[3])], axis=1
            )

        high, low = stacked(left_hi), stacked(left_lo)
        total = jnp.dot(high, win_hi[...], preferred_element_type=F32)
        total += jnp.dot(high, win_lo[...], preferred_element_type=F32)
        total += jnp.dot(low, win_hi[...], preferred_element_type=F32)
        down_out[step] = total[0:B]
        middle[step] = total[B : 2 * B]
        up_out[step] = total[2 * B : 3 * B]

    def send_up(turn, n):
        step = 2 * order[turn] + n

        def start(n, direct):
            if direct:
                halo_copy(step, 0).start()
            else:
                pass_copy(step, 2 * turn + n).start()

        up_either(turn, start, (n,))

    def up_either(turn, act, which):
        if far and 2 * turn < DETOURS:

            @pl.when(is_last)
            def _():
                for n in which:
                    act(n, False)

            @pl.when(jnp.logical_not(is_last))
            def _():
                for n in which:
                    act(n, True)
        else:
            for n in which:
                act(n, True)

    def pass_on(turn):
        if far:

            @pl.when(is_passer)
            def _():
                for n in range(2):
                    step = 2 * order[turn] + n
                    pass_copy(step, 2 * turn + n).wait_recv()
                    on_copy(step, 2 * turn + n).start()

    def send_down(step):
        halo_copy(step, 1).start()

    def finish(step):
        halo_copy(step, 0).wait_recv()
        halo_copy(step, 1).wait_recv()
        for e in range(5):
            parts = []
            for ref, shift in ((lower, 0), (middle, 1), (upper, 2)):
                if 0 <= e - shift < 3:
                    parts.append(ref[step, :, (e - shift) * 2 * B : (e - shift + 1) * 2 * B])
            column = pl.multiple_of(e * NX * NY * B + step * 2 * B, 2 * B)
            out_ref[:, pl.ds(column, 2 * B)] = sum(parts[1:], parts[0])

    def both_steps(turn, work):
        def one(n, carry):
            work(2 * order[turn] + n)
            return carry

        lax.fori_loop(0, 2, one, 0)

    def multiply(turn):
        def one(n, carry):
            step = 2 * order[turn] + n
            compute(step)
            send_up(turn, n)
            if turn == 0:

                @pl.when(jnp.logical_not(is_first))
                def _():
                    send_down(step)
            else:
                send_down(step)
            return carry

        lax.fori_loop(0, 2, one, 0)

    def unless_patient(condition, turn):
        if far:
            condition = condition & jnp.logical_not(is_patient)

        @pl.when(condition)
        def _():
            y_take(turn)

    inputs[4].wait()
    lax.fori_loop(0, 2, left_product, 0)
    for shift in range(1, NX):
        ask_landing(shift).wait_recv()
    if far:

        @pl.when(is_patient)
        def _():
            for turn in range(1, 4):
                y_take(turn)
            pl.semaphore_wait(ready.at[2], 1)

    serve(0)
    lax.fori_loop(2, 3, left_product, 0)
    unless_patient(y >= 0, 1)
    serve(1)
    lax.fori_loop(3, 4, left_product, 0)
    unless_patient(y >= 0, 2)
    serve(2)
    unless_patient(jnp.logical_not(is_end), 3)
    x_take(0)

    @pl.when(jnp.logical_not(is_last))
    def _():
        pl.semaphore_wait(ready.at[0], 1)

    multiply(0)
    unless_patient(is_end, 3)
    serve(3)
    if far:

        @pl.when(is_last)
        def _():
            signal(ready.at[2], (blk, below))

    x_take(1)

    @pl.when(is_first)
    def _():
        pl.semaphore_wait(ready.at[1], 1)
        both_steps(0, send_down)

    multiply(1)
    pass_on(0)
    x_take(2)
    multiply(2)
    pass_on(1)
    x_take(3)
    multiply(3)
    for turn in range(4):
        both_steps(turn, finish)

    for n, jump in enumerate((1, -1, 2, -2)):

        @pl.when(inside(y + jump))
        def _():
            y_copy(y, y + jump, n).wait_send()

    @pl.when(jnp.logical_not(is_end))
    def _():
        y_copy(3 - hand_target, hand_target, 4).wait_send()

    for shift in range(1, NX):
        ask_copy(shift).wait_send()

    def drain_x(source, carry):
        for shift in range(1, NX):
            x_copy(source, shift).wait_send()
        return carry

    lax.fori_loop(0, NY, drain_x, 0)

    def drain_halo(step, carry):
        halo_copy(step, 1).wait_send()
        return carry

    lax.fori_loop(0, STEPS, drain_halo, 0)
    for turn in range(4):

        def drain_up(n, direct, turn=turn):
            step = 2 * order[turn] + n
            if direct:
                halo_copy(step, 0).wait_send()
            else:
                pass_copy(step, 2 * turn + n).wait_send()

        up_either(turn, drain_up, (0, 1))
    if far:

        @pl.when(is_passer)
        def _():
            for n in range(DETOURS):
                on_copy(2 * order[n // 2] + n % 2, n).wait_send()


def body(fine_blocks, source_group, source_row, prolong_blocks, prolong_code):
    hbm = pl.BlockSpec(memory_space=pltpu.HBM)
    window = 3 * 2 * B
    halo = pltpu.VMEM((STEPS, B, window), F32)
    dma = pltpu.SemaphoreType.DMA
    return pl.pallas_call(
        kernel,
        out_shape=jax.ShapeDtypeStruct((B, 5 * NX * NY * B), F32),
        in_specs=[hbm] * 5,
        out_specs=pl.BlockSpec(memory_space=pltpu.VMEM),
        scratch_shapes=[
            pltpu.VMEM((FB, B, KA * B), F32),
            pltpu.SMEM((FB, KA), jnp.int32),
            pltpu.SMEM((FB, KA), jnp.int32),
            pltpu.SMEM((2, FB), jnp.int32),
            pltpu.VMEM((NY, PACK, 2 * B), F32),
            pltpu.VMEM((NX, NY * MB, 2 * B), F32),
            pltpu.VMEM((NX, NY * MB, 2 * B), F32),
            pltpu.VMEM((NX, NY, SHARE, 2 * B), F32),
            pltpu.VMEM((NX, NY, SHARE, 2 * B), F32),
            pltpu.VMEM((FB * KA, 3 * B, 2 * B), BF16),
            pltpu.VMEM((FB * KA, 3 * B, 2 * B), BF16),
            pltpu.VMEM((2 * MB * B, window), BF16),
            pltpu.VMEM((2 * MB * B, window), BF16),
            halo, halo, halo, halo, halo,
            pltpu.VMEM((DETOURS, B, window), F32),
            pltpu.SMEM((MB * NX * NY,), jnp.int32),
            dma((5,)),
            dma((5,)), dma((NY,)),
            dma((NX,)), dma((NX,)),
            dma((NX, NY)), dma((NX, NY)),
            dma((2, STEPS)), dma((2, STEPS)),
            dma((DETOURS,)), dma((DETOURS,)), dma((DETOURS,)),
            pltpu.SemaphoreType.REGULAR((3,)),
        ],
        compiler_params=pltpu.CompilerParams(
            collective_id=0, has_side_effects=True, vmem_limit_bytes=40 * 2**20
        ),
        cost_estimate=pl.CostEstimate(flops=10**9, bytes_accessed=4 * 2**20, transcendentals=0),
        name="galerkin",
    )(*[
        pltpu.with_memory_space_constraint(each, pltpu.HBM)
        for each in (fine_blocks, prolong_blocks.reshape(FB * B, 2 * B), source_group, source_row, prolong_code.T)
    ])


def solution(mesh):
    return jax.shard_map(
        body,
        mesh=mesh,
        in_specs=(
            P(("blk", "band"), None, None),
            P(("blk", "band"), None),
            P(("blk", "band"), None),
            P(("blk", "band"), None, None),
            P(("blk", "band"), None),
        ),
        out_specs=P(("blk", "band"), None),
        check_vma=False,
    )
```

```python
import jax
import jax.numpy as jnp
from jax import lax
from jax.experimental import pallas as pl
from jax.experimental.pallas import tpu as pltpu
from jax.sharding import PartitionSpec as P

MESH = pl.DeviceIdType.MESH
F32 = jnp.float32
BF16 = jnp.bfloat16

B = 64
FB = 4
KA = 4
MB = 2
NX = 4
NY = 4
PACK = FB * B + 8
SHARE = MB * B + 8
STEPS = NX * NY // 2
DETOURS = (4, 2)
HEAD = 136


def kernel(
    a_hbm, p_hbm, group_hbm, row_hbm, code_hbm, out_ref,
    a_ref, group_ref, row_ref, code_ref,
    held, want, asked, staged, got, left_hi, left_lo, win_hi, win_lo,
    middle, up_out, down_out, lower, upper, passing, pair_tab,
    in_sem, y_send, y_recv, ask_send, ask_recv, x_send, x_recv, halo_send, halo_recv,
    pass_send, pass_recv, on_send, ready,
):
    blk, band = lax.axis_index("blk"), lax.axis_index("band")
    bands = lax.axis_size("band")
    half_bands = bands // 2
    y, x = blk // NX, blk % NX
    above, below = (band + 1) % bands, (band + bands - 1) % bands
    place = band % half_bands
    is_first, is_last = place == 0, place == half_bands - 1
    far = half_bands >= 4
    is_patient, is_passer = place == half_bands - 2, (place == half_bands - 3, place == 2)
    lane = lax.broadcasted_iota(jnp.int32, (B, 2 * B), 1)
    first_half = lane < B

    def at(row, column):
        return (row * NX + column, band)

    def inside(row):
        return (row >= 0) & (row < NY)

    def beside(shift):
        return (x + shift) % NX

    def signal(semaphore, target):
        pl.semaphore_signal(semaphore, inc=1, device_id=target, device_id_type=MESH)

    inputs = [
        pltpu.make_async_copy(source, target, in_sem.at[n])
        for n, (source, target) in enumerate((
            (group_hbm, group_ref), (row_hbm, row_ref), (code_hbm, code_ref),
            (p_hbm, held.at[y, pl.ds(0, FB * B)]), (a_hbm, a_ref),
        ))
    ]
    for copy in inputs:
        copy.start()

    barrier = pltpu.get_barrier_semaphore()
    for shift in range(1, NX):
        signal(barrier, at(y, beside(shift)))

    for jump in (1, -1, 2, -2):

        @pl.when(inside(y + jump))
        def _():
            signal(barrier, at(y + jump, x))

    @pl.when(jnp.logical_not(is_last))
    def _():
        signal(barrier, (blk, above))

    @pl.when(is_first)
    def _():
        signal(barrier, (blk, below))
        if far:
            signal(barrier, (blk, (band + bands - 3) % bands))
            signal(barrier, (blk, band + 2))

    if far:

        @pl.when(is_passer[0])
        def _():
            signal(barrier, (blk, band + 2))

        @pl.when(is_passer[1])
        def _():
            signal(barrier, (blk, (band + bands - 3) % bands))

    inputs[2].wait()
    tile_row = lax.broadcasted_iota(jnp.int32, (8, 2 * B), 0)
    tile_lane = lax.broadcasted_iota(jnp.int32, (8, 2 * B), 1)
    codes = jnp.zeros((8, 2 * B), F32)
    for i in range(FB):
        one = jnp.where(tile_lane < B, code_ref[0, i], code_ref[1, i]).astype(F32)
        codes = jnp.where(tile_row == i, one, codes)
    held[y, FB * B : PACK, :] = codes
    inputs[3].wait()

    pl.semaphore_wait(
        barrier,
        NX - 1 + sum(jnp.where(inside(y + jump), 1, 0) for jump in (1, -1, 2, -2))
        + jnp.where(is_first, 0, 1) + jnp.where(is_last, 3 if far else 1, 0)
        + (jnp.where(is_passer[0] | is_passer[1], 1, 0) if far else 0),
    )

    def y_copy(source, target, sender, part=None):
        rows = pl.ds(0, PACK) if part is None else (pl.ds(0, HEAD), pl.ds(HEAD, PACK - HEAD))[part]
        slot = held.at[source, rows]
        return pltpu.make_async_remote_copy(
            src_ref=slot, dst_ref=slot, send_sem=y_send.at[sender], recv_sem=y_recv.at[part or 0, source],
            device_id=at(target, x), device_id_type=MESH,
        )

    def ask_copy(shift):
        return pltpu.make_async_remote_copy(
            src_ref=want.at[beside(shift)], dst_ref=asked.at[NX - shift],
            send_sem=ask_send.at[shift], recv_sem=ask_recv.at[NX - shift],
            device_id=at(y, beside(shift)), device_id_type=MESH,
        )

    def x_copy(source, shift):
        return pltpu.make_async_remote_copy(
            src_ref=staged.at[shift, source], dst_ref=got.at[x, source],
            send_sem=x_send.at[shift, source], recv_sem=x_recv.at[shift, source],
            device_id=at(y, beside(shift)), device_id_type=MESH,
        )

    def x_landing(source, shift):
        return pltpu.make_async_remote_copy(
            src_ref=staged.at[shift, source], dst_ref=got.at[beside(NX - shift), source],
            send_sem=x_send.at[shift, source], recv_sem=x_recv.at[shift, source],
            device_id=at(y, beside(shift)), device_id_type=MESH,
        )

    def ask_landing(shift):
        return pltpu.make_async_remote_copy(
            src_ref=want.at[beside(shift)], dst_ref=asked.at[shift],
            send_sem=ask_send.at[shift], recv_sem=ask_recv.at[shift],
            device_id=at(y, beside(shift)), device_id_type=MESH,
        )

    def halo_copy(step, side):
        return pltpu.make_async_remote_copy(
            src_ref=(down_out if side else up_out).at[step], dst_ref=(upper if side else lower).at[step],
            send_sem=halo_send.at[side, step], recv_sem=halo_recv.at[side, step],
            device_id=(blk, below if side else above), device_id_type=MESH,
        )

    def pass_copy(side, step, n):
        return pltpu.make_async_remote_copy(
            src_ref=(down_out if side else up_out).at[step], dst_ref=passing.at[side, n],
            send_sem=pass_send.at[side, n], recv_sem=pass_recv.at[side, n],
            device_id=(blk, (band + (2 if side else bands - 2)) % bands), device_id_type=MESH,
        )

    def on_copy(side, step, n):
        return pltpu.make_async_remote_copy(
            src_ref=passing.at[side, n], dst_ref=(upper if side else lower).at[step],
            send_sem=on_send.at[side, n], recv_sem=halo_recv.at[side, step],
            device_id=(blk, (band + (bands - 3 if side else 3)) % bands), device_id_type=MESH,
        )

    order = [
        y,
        jnp.where(y == 0, 1, y - 1),
        jnp.where(y == 0, 2, jnp.where(y == 3, 1, y + 1)),
        jnp.where(y < 2, 3, 0),
    ]

    is_end = (y == 0) | (y == NY - 1)
    end_jump = jnp.where(y == 0, 1, -1)
    inner_jump = jnp.where(y == 1, 1, -1)
    hand_source, hand_target = jnp.where(y == 1, 3, 0), jnp.where(y == 1, 0, 3)

    def y_sends(act):
        @pl.when(is_end)
        def _():
            act(y_copy(y, y + 2 * end_jump, 0, 0))
            act(y_copy(y, y + 2 * end_jump, 1, 1))
            act(y_copy(y, y + end_jump, 2))

        @pl.when(jnp.logical_not(is_end))
        def _():
            act(y_copy(y, y + inner_jump, 2))
            act(y_copy(y, y - inner_jump, 3))
            act(y_copy(y, y + 2 * inner_jump, 0))

    def hand_on(part):
        return y_copy(hand_source, hand_target, 4 + part, part)

    def serve(turn):
        source = order[turn]

        def choose(wanted, slot, target):
            row = wanted(MB * source + slot)
            pick = jnp.broadcast_to(row, (B, 2 * B))
            values = jnp.zeros((B, 2 * B), F32)
            code = jnp.zeros((1, 2 * B), F32)
            for i in range(FB):
                values = jnp.where(pick == i, held[source, i * B : (i + 1) * B, :], values)
                code = jnp.where(row == i, held[source, FB * B + i : FB * B + i + 1, :], code)
            target(slice(slot * B, (slot + 1) * B), values)
            target(slice(MB * B + slot, MB * B + slot + 1), code)

        for shift in (2, 1, 3):
            for slot in range(MB):

                def wanted(n, shift=shift):
                    return asked[shift, pl.ds(n, 1), :]

                def target(rows, values, shift=shift):
                    staged[shift, source, rows, :] = values

                choose(wanted, slot, target)
            x_copy(source, shift).start()
        for slot in range(MB):

            def own(n):
                return want[x, pl.ds(n, 1), :]

            def keep(rows, values):
                got[x, source, rows, :] = values

            choose(own, slot, keep)

    def y_take(turn):
        source = order[turn]
        sender = jnp.where(source < y, y - 1, y + 1)
        if turn < 3:
            y_copy(source, sender, 0).wait_recv()
            return
        for part in range(2):
            y_copy(source, sender, 0, part).wait_recv()

            @pl.when(jnp.logical_not(is_end))
            def _():
                hand_on(part).start()

    def x_take(turn):
        for shift in range(1, NX):
            x_landing(order[turn], shift).wait_recv()

    @pl.when(jnp.logical_not(is_first))
    def _():
        signal(ready.at[0], (blk, below))

    @pl.when(is_last)
    def _():
        signal(ready.at[1], (blk, above))
        if far:
            signal(ready.at[4], (blk, (band + 3) % bands))

    if far:

        @pl.when(is_passer[1])
        def _():
            signal(ready.at[3], (blk, band - 2))

        @pl.when(is_patient)
        def _():
            pl.semaphore_wait(ready.at[2], 1)

    y_sends(lambda copy: copy.start())

    for copy in inputs[0:2]:
        copy.wait()

    def tabulate(group, carry):
        pair = [jnp.int32(0), jnp.int32(0)]
        row = [jnp.int32(FB), jnp.int32(FB)]
        for at_pair in range(FB * KA - 1, -1, -1):
            i, k = at_pair // KA, at_pair % KA
            hit = group_ref[i, k] == group
            pair = [jnp.where(hit, at_pair, pair[0]), jnp.where(hit, pair[0], pair[1])]
            row = [jnp.where(hit, row_ref[i, k], row[0]), jnp.where(hit, row[0], row[1])]
        for slot in range(MB):
            pair_tab[MB * group + slot] = pair[slot]
            want[group % NX, pl.ds(MB * (group // NX) + slot, 1), :] = jnp.full((1, 2 * B), row[slot]).astype(F32)
        return carry

    lax.fori_loop(0, NX * NY, tabulate, 0)

    for shift in (2, 1, 3):
        ask_copy(shift).start()

    def windowed(values, code, at_code):
        chosen = jnp.where(code == at_code, values, 0.0)
        return chosen + pltpu.roll(chosen, B, 1)

    def left_product(i, carry):
        p_here = held[y, pl.ds(pl.multiple_of(i * B, B), B), :]
        code = jnp.broadcast_to(held[y, pl.ds(FB * B + i, 1), :], (B, 2 * B))
        parts = [windowed(p_here, code, d) for d in range(3)]
        restrict = jnp.concatenate(
            [jnp.where(first_half, parts[0], parts[1]), jnp.where(first_half, parts[2], 0.0)], axis=1
        )
        twice = []
        for side in range(2):
            both = a_ref[i, :, side * 2 * B : (side + 1) * 2 * B]
            turned = pltpu.roll(both, B, 1)
            twice += [jnp.where(first_half, both, turned), jnp.where(first_half, turned, both)]
        result = lax.dot_general(
            restrict, jnp.concatenate(twice, axis=1), (((0,), (0,)), ((), ())),
            precision=lax.Precision.HIGHEST, preferred_element_type=F32,
        )[0 : 3 * B]
        high = result.astype(BF16)
        low = (result - high.astype(F32)).astype(BF16)
        for k in range(KA):
            left_hi[i * KA + k] = high[:, k * 2 * B : (k + 1) * 2 * B]
            left_lo[i * KA + k] = low[:, k * 2 * B : (k + 1) * 2 * B]
        return carry

    wide_half = lax.broadcasted_iota(jnp.int32, (3 * B, 2 * B), 1) < B

    def compute(step):
        for half in range(2):
            row, column = step // 2, 2 * (step % 2) + half
            for slot in range(MB):
                values = got[column, row, slot * B : (slot + 1) * B, :]
                code = jnp.broadcast_to(got[column, row, MB * B + slot : MB * B + slot + 1, :], (B, 2 * B))
                mine = first_half if half == 0 else jnp.logical_not(first_half)
                at_row = (MB * half + slot) * B
                for e in range(3):
                    part = jnp.where(mine, windowed(values, code, e), 0.0)
                    high = part.astype(BF16)
                    win_hi[at_row : at_row + B, e * 2 * B : (e + 1) * 2 * B] = high
                    win_lo[at_row : at_row + B, e * 2 * B : (e + 1) * 2 * B] = (part - high.astype(F32)).astype(BF16)

        def stacked(ref):
            pairs = [ref[pair_tab[2 * MB * step + n]] for n in range(2 * MB)]
            return jnp.concatenate(
                [jnp.where(wide_half, pairs[0], pairs[1]), jnp.where(wide_half, pairs[2], pairs[3])], axis=1
            )

        high, low = stacked(left_hi), stacked(left_lo)
        total = jnp.dot(high, win_hi[...], preferred_element_type=F32)
        total += jnp.dot(high, win_lo[...], preferred_element_type=F32)
        total += jnp.dot(low, win_hi[...], preferred_element_type=F32)
        down_out[step] = total[0:B]
        middle[step] = total[B : 2 * B]
        up_out[step] = total[2 * B : 3 * B]

    def detour(side, turn, n):
        if side == 0:
            return is_last & (n == 1), turn
        return is_first & (turn == 0), n

    def each_way(side, turn, n, act):
        step = 2 * order[turn] + n
        if not far or (side and turn):
            act(halo_copy(step, side))
            return
        around, index = detour(side, turn, n)

        @pl.when(around)
        def _():
            act(pass_copy(side, step, index))

        @pl.when(jnp.logical_not(around))
        def _():
            act(halo_copy(step, side))

    def passed_on(side, turn):
        return [(2 * order[turn] + 1, turn)] if side == 0 else [(2 * order[turn] + n, n) for n in range(2 - 2 * min(turn, 1))]

    def pass_on(turn):
        for side in range(2):
            if far and passed_on(side, turn):

                @pl.when(is_passer[side])
                def _():
                    if side:
                        pl.semaphore_wait(ready.at[4], 1)
                    for step, index in passed_on(side, turn):
                        pass_copy(side, step, index).wait_recv()
                        on_copy(side, step, index).start()

    def finish(step):
        halo_copy(step, 0).wait_recv()
        halo_copy(step, 1).wait_recv()
        for e in range(5):
            parts = []
            for ref, shift in ((lower, 0), (middle, 1), (upper, 2)):
                if 0 <= e - shift < 3:
                    parts.append(ref[step, :, (e - shift) * 2 * B : (e - shift + 1) * 2 * B])
            column = pl.multiple_of(e * NX * NY * B + step * 2 * B, 2 * B)
            out_ref[:, pl.ds(column, 2 * B)] = sum(parts[1:], parts[0])

    def both_steps(turn, work):
        def one(n, carry):
            work(2 * order[turn] + n)
            return carry

        lax.fori_loop(0, 2, one, 0)

    def multiply(turn):
        def one(n, carry):
            compute(2 * order[turn] + n)
            for side in range(2):
                each_way(side, turn, n, lambda copy: copy.start())
            return carry

        lax.fori_loop(0, 2, one, 0)

    inputs[4].wait()
    lax.fori_loop(0, 2, left_product, 0)
    for shift in range(1, NX):
        ask_landing(shift).wait_recv()
    serve(0)
    lax.fori_loop(2, 3, left_product, 0)
    y_take(1)
    serve(1)
    lax.fori_loop(3, 4, left_product, 0)
    y_take(2)
    serve(2)

    @pl.when(jnp.logical_not(is_end))
    def _():
        y_take(3)

    x_take(0)

    @pl.when(jnp.logical_not(is_last))
    def _():
        pl.semaphore_wait(ready.at[0], 1)

    @pl.when(is_first)
    def _():
        pl.semaphore_wait(ready.at[3 if far else 1], 1)

    multiply(0)

    @pl.when(is_end)
    def _():
        y_take(3)

    if far:

        @pl.when(is_last)
        def _():
            signal(ready.at[2], (blk, below))

    serve(3)
    x_take(1)
    if far:

        @pl.when(is_first)
        def _():
            pl.semaphore_wait(ready.at[1], 1)

    multiply(1)
    pass_on(0)
    x_take(2)
    multiply(2)
    pass_on(1)
    x_take(3)
    multiply(3)
    pass_on(2)
    pass_on(3)
    for turn in range(4):
        both_steps(turn, finish)

    y_sends(lambda copy: copy.wait_send())

    @pl.when(jnp.logical_not(is_end))
    def _():
        hand_on(0).wait_send()
        hand_on(1).wait_send()

    for shift in range(1, NX):
        ask_copy(shift).wait_send()

    def drain_x(source, carry):
        for shift in range(1, NX):
            x_copy(source, shift).wait_send()
        return carry

    lax.fori_loop(0, NY, drain_x, 0)

    for side in range(2):
        for turn in range(4):
            for n in range(2):
                each_way(side, turn, n, lambda copy: copy.wait_send())
            if far and passed_on(side, turn):

                @pl.when(is_passer[side])
                def _():
                    for step, index in passed_on(side, turn):
                        on_copy(side, step, index).wait_send()


def body(fine_blocks, source_group, source_row, prolong_blocks, prolong_code):
    hbm = pl.BlockSpec(memory_space=pltpu.HBM)
    window = 3 * 2 * B
    halo = pltpu.VMEM((STEPS, B, window), F32)
    dma = pltpu.SemaphoreType.DMA
    return pl.pallas_call(
        kernel,
        out_shape=jax.ShapeDtypeStruct((B, 5 * NX * NY * B), F32),
        in_specs=[hbm] * 5,
        out_specs=pl.BlockSpec(memory_space=pltpu.VMEM),
        scratch_shapes=[
            pltpu.VMEM((FB, B, KA * B), F32),
            pltpu.SMEM((FB, KA), jnp.int32),
            pltpu.SMEM((FB, KA), jnp.int32),
            pltpu.SMEM((2, FB), jnp.int32),
            pltpu.VMEM((NY, PACK, 2 * B), F32),
            pltpu.VMEM((NX, NY * MB, 2 * B), F32),
            pltpu.VMEM((NX, NY * MB, 2 * B), F32),
            pltpu.VMEM((NX, NY, SHARE, 2 * B), F32),
            pltpu.VMEM((NX, NY, SHARE, 2 * B), F32),
            pltpu.VMEM((FB * KA, 3 * B, 2 * B), BF16),
            pltpu.VMEM((FB * KA, 3 * B, 2 * B), BF16),
            pltpu.VMEM((2 * MB * B, window), BF16),
            pltpu.VMEM((2 * MB * B, window), BF16),
            halo, halo, halo, halo, halo,
            pltpu.VMEM((2, max(DETOURS), B, window), F32),
            pltpu.SMEM((MB * NX * NY,), jnp.int32),
            dma((5,)),
            dma((6,)), dma((2, NY)),
            dma((NX,)), dma((NX,)),
            dma((NX, NY)), dma((NX, NY)),
            dma((2, STEPS)), dma((2, STEPS)),
            dma((2, max(DETOURS))), dma((2, max(DETOURS))), dma((2, max(DETOURS))),
            pltpu.SemaphoreType.REGULAR((5,)),
        ],
        compiler_params=pltpu.CompilerParams(
            collective_id=0, has_side_effects=True, vmem_limit_bytes=40 * 2**20
        ),
        cost_estimate=pl.CostEstimate(flops=10**9, bytes_accessed=4 * 2**20, transcendentals=0),
        name="galerkin",
    )(*[
        pltpu.with_memory_space_constraint(each, pltpu.HBM)
        for each in (fine_blocks, prolong_blocks.reshape(FB * B, 2 * B), source_group, source_row, prolong_code.T)
    ])


def solution(mesh):
    return jax.shard_map(
        body,
        mesh=mesh,
        in_specs=(
            P(("blk", "band"), None, None),
            P(("blk", "band"), None),
            P(("blk", "band"), None),
            P(("blk", "band"), None, None),
            P(("blk", "band"), None),
        ),
        out_specs=P(("blk", "band"), None),
        check_vma=False,
    )
```

```python
import jax
import jax.numpy as jnp
from jax import lax
from jax.experimental import pallas as pl
from jax.experimental.pallas import tpu as pltpu
from jax.sharding import PartitionSpec as P

MESH = pl.DeviceIdType.MESH
F32 = jnp.float32
BF16 = jnp.bfloat16

B = 64
FB = 4
KA = 4
MB = 2
NX = 4
NY = 4
PACK = FB * B + 8
SHARE = MB * B + 8
STEPS = NX * NY // 2
DETOURS = (4, 2)
HEAD = 136


def kernel(
    a_hbm, p_hbm, group_hbm, row_hbm, code_hbm, out_ref,
    a_ref, group_ref, row_ref, code_ref,
    held, want, asked, staged, got, left_hi, left_lo, win_hi, win_lo,
    middle, up_out, down_out, lower, upper, passing, pair_tab,
    in_sem, y_send, y_recv, ask_send, ask_recv, x_send, x_recv, halo_send, halo_recv,
    pass_send, pass_recv, on_send, ready,
):
    blk, band = lax.axis_index("blk"), lax.axis_index("band")
    bands = lax.axis_size("band")
    half_bands = bands // 2
    y, x = blk // NX, blk % NX
    above, below = (band + 1) % bands, (band + bands - 1) % bands
    place = band % half_bands
    is_first, is_last = place == 0, place == half_bands - 1
    far = half_bands >= 4
    is_patient, is_passer = place == half_bands - 2, (place == half_bands - 3, place == 2)
    lane = lax.broadcasted_iota(jnp.int32, (B, 2 * B), 1)
    first_half = lane < B

    def at(row, column):
        return (row * NX + column, band)

    def inside(row):
        return (row >= 0) & (row < NY)

    def beside(shift):
        return (x + shift) % NX

    def signal(semaphore, target):
        pl.semaphore_signal(semaphore, inc=1, device_id=target, device_id_type=MESH)

    inputs = [
        pltpu.make_async_copy(source, target, in_sem.at[n])
        for n, (source, target) in enumerate((
            (group_hbm, group_ref), (row_hbm, row_ref), (code_hbm, code_ref),
            (p_hbm, held.at[y, pl.ds(0, FB * B)]), (a_hbm, a_ref),
        ))
    ]
    for copy in inputs:
        copy.start()

    barrier = pltpu.get_barrier_semaphore()
    for shift in range(1, NX):
        signal(barrier, at(y, beside(shift)))

    for jump in (1, -1, 2, -2):

        @pl.when(inside(y + jump))
        def _():
            signal(barrier, at(y + jump, x))

    @pl.when(jnp.logical_not(is_last))
    def _():
        signal(barrier, (blk, above))

    @pl.when(is_first)
    def _():
        signal(barrier, (blk, below))
        if far:
            signal(barrier, (blk, (band + bands - 3) % bands))
            signal(barrier, (blk, band + 2))

    if far:

        @pl.when(is_passer[0])
        def _():
            signal(barrier, (blk, band + 2))

        @pl.when(is_passer[1])
        def _():
            signal(barrier, (blk, (band + bands - 3) % bands))

    inputs[2].wait()
    tile_row = lax.broadcasted_iota(jnp.int32, (8, 2 * B), 0)
    tile_lane = lax.broadcasted_iota(jnp.int32, (8, 2 * B), 1)
    codes = jnp.zeros((8, 2 * B), F32)
    for i in range(FB):
        one = jnp.where(tile_lane < B, code_ref[0, i], code_ref[1, i]).astype(F32)
        codes = jnp.where(tile_row == i, one, codes)
    held[y, FB * B : PACK, :] = codes
    inputs[3].wait()

    pl.semaphore_wait(
        barrier,
        NX - 1 + sum(jnp.where(inside(y + jump), 1, 0) for jump in (1, -1, 2, -2))
        + jnp.where(is_first, 0, 1) + jnp.where(is_last, 3 if far else 1, 0)
        + (jnp.where(is_passer[0] | is_passer[1], 1, 0) if far else 0),
    )

    def y_copy(source, target, sender, part=None):
        rows = pl.ds(0, PACK) if part is None else (pl.ds(0, HEAD), pl.ds(HEAD, PACK - HEAD))[part]
        slot = held.at[source, rows]
        return pltpu.make_async_remote_copy(
            src_ref=slot, dst_ref=slot, send_sem=y_send.at[sender], recv_sem=y_recv.at[part or 0, source],
            device_id=at(target, x), device_id_type=MESH,
        )

    def ask_copy(shift):
        return pltpu.make_async_remote_copy(
            src_ref=want.at[beside(shift)], dst_ref=asked.at[NX - shift],
            send_sem=ask_send.at[shift], recv_sem=ask_recv.at[NX - shift],
            device_id=at(y, beside(shift)), device_id_type=MESH,
        )

    def x_copy(source, shift):
        return pltpu.make_async_remote_copy(
            src_ref=staged.at[shift, source], dst_ref=got.at[x, source],
            send_sem=x_send.at[shift, source], recv_sem=x_recv.at[shift, source],
            device_id=at(y, beside(shift)), device_id_type=MESH,
        )

    def x_landing(source, shift):
        return pltpu.make_async_remote_copy(
            src_ref=staged.at[shift, source], dst_ref=got.at[beside(NX - shift), source],
            send_sem=x_send.at[shift, source], recv_sem=x_recv.at[shift, source],
            device_id=at(y, beside(shift)), device_id_type=MESH,
        )

    def ask_landing(shift):
        return pltpu.make_async_remote_copy(
            src_ref=want.at[beside(shift)], dst_ref=asked.at[shift],
            send_sem=ask_send.at[shift], recv_sem=ask_recv.at[shift],
            device_id=at(y, beside(shift)), device_id_type=MESH,
        )

    def halo_copy(step, side):
        return pltpu.make_async_remote_copy(
            src_ref=(down_out if side else up_out).at[step], dst_ref=(upper if side else lower).at[step],
            send_sem=halo_send.at[side, step], recv_sem=halo_recv.at[side, step],
            device_id=(blk, below if side else above), device_id_type=MESH,
        )

    def pass_copy(side, step, n):
        return pltpu.make_async_remote_copy(
            src_ref=(down_out if side else up_out).at[step], dst_ref=passing.at[side, n],
            send_sem=pass_send.at[side, n], recv_sem=pass_recv.at[side, n],
            device_id=(blk, (band + (2 if side else bands - 2)) % bands), device_id_type=MESH,
        )

    def on_copy(side, step, n):
        return pltpu.make_async_remote_copy(
            src_ref=passing.at[side, n], dst_ref=(upper if side else lower).at[step],
            send_sem=on_send.at[side, n], recv_sem=halo_recv.at[side, step],
            device_id=(blk, (band + (bands - 3 if side else 3)) % bands), device_id_type=MESH,
        )

    order = [
        y,
        jnp.where(y == 0, 1, y - 1),
        jnp.where(y == 0, 2, jnp.where(y == 3, 1, y + 1)),
        jnp.where(y < 2, 3, 0),
    ]

    is_end = (y == 0) | (y == NY - 1)
    end_jump = jnp.where(y == 0, 1, -1)
    inner_jump = jnp.where(y == 1, 1, -1)
    hand_source, hand_target = jnp.where(y == 1, 3, 0), jnp.where(y == 1, 0, 3)

    def y_sends(act):
        @pl.when(is_end)
        def _():
            act(y_copy(y, y + 2 * end_jump, 0, 0))
            act(y_copy(y, y + 2 * end_jump, 1, 1))
            act(y_copy(y, y + end_jump, 2))

        @pl.when(jnp.logical_not(is_end))
        def _():
            act(y_copy(y, y + inner_jump, 2))
            act(y_copy(y, y - inner_jump, 3))
            act(y_copy(y, y + 2 * inner_jump, 0))

    def hand_on(part):
        return y_copy(hand_source, hand_target, 4 + part, part)

    def serve(turn):
        source = order[turn]

        def choose(wanted, slot, target):
            row = wanted(MB * source + slot)
            pick = jnp.broadcast_to(row, (B, 2 * B))
            values = jnp.zeros((B, 2 * B), F32)
            code = jnp.zeros((1, 2 * B), F32)
            for i in range(FB):
                values = jnp.where(pick == i, held[source, i * B : (i + 1) * B, :], values)
                code = jnp.where(row == i, held[source, FB * B + i : FB * B + i + 1, :], code)
            target(slice(slot * B, (slot + 1) * B), values)
            target(slice(MB * B + slot, MB * B + slot + 1), code)

        for shift in (2, 1, 3):
            for slot in range(MB):

                def wanted(n, shift=shift):
                    return asked[shift, pl.ds(n, 1), :]

                def target(rows, values, shift=shift):
                    staged[shift, source, rows, :] = values

                choose(wanted, slot, target)
            x_copy(source, shift).start()
        for slot in range(MB):

            def own(n):
                return want[x, pl.ds(n, 1), :]

            def keep(rows, values):
                got[x, source, rows, :] = values

            choose(own, slot, keep)

    def y_take(turn):
        source = order[turn]
        sender = jnp.where(source < y, y - 1, y + 1)
        if turn < 3:
            y_copy(source, sender, 0).wait_recv()
            return
        for part in range(2):
            y_copy(source, sender, 0, part).wait_recv()

            @pl.when(jnp.logical_not(is_end))
            def _():
                hand_on(part).start()

    def x_take(turn):
        for shift in range(1, NX):
            x_landing(order[turn], shift).wait_recv()

    @pl.when(jnp.logical_not(is_first))
    def _():
        signal(ready.at[0], (blk, below))

    @pl.when(is_last)
    def _():
        signal(ready.at[1], (blk, above))
        if far:
            signal(ready.at[4], (blk, (band + 3) % bands))

    if far:

        @pl.when(is_passer[1])
        def _():
            signal(ready.at[3], (blk, band - 2))

        @pl.when(is_patient)
        def _():
            pl.semaphore_wait(ready.at[2], 1)

    y_sends(lambda copy: copy.start())

    for copy in inputs[0:2]:
        copy.wait()

    def tabulate(group, carry):
        pair = [jnp.int32(0), jnp.int32(0)]
        row = [jnp.int32(FB), jnp.int32(FB)]
        for at_pair in range(FB * KA - 1, -1, -1):
            i, k = at_pair // KA, at_pair % KA
            hit = group_ref[i, k] == group
            pair = [jnp.where(hit, at_pair, pair[0]), jnp.where(hit, pair[0], pair[1])]
            row = [jnp.where(hit, row_ref[i, k], row[0]), jnp.where(hit, row[0], row[1])]
        for slot in range(MB):
            pair_tab[MB * group + slot] = pair[slot]
            want[group % NX, pl.ds(MB * (group // NX) + slot, 1), :] = jnp.full((1, 2 * B), row[slot]).astype(F32)
        return carry

    lax.fori_loop(0, NX * NY, tabulate, 0)

    for shift in (2, 1, 3):
        ask_copy(shift).start()

    def windowed(values, code, at_code):
        chosen = jnp.where(code == at_code, values, 0.0)
        return chosen + pltpu.roll(chosen, B, 1)

    def left_product(i, carry):
        p_here = held[y, pl.ds(pl.multiple_of(i * B, B), B), :]
        code = jnp.broadcast_to(held[y, pl.ds(FB * B + i, 1), :], (B, 2 * B))
        parts = [windowed(p_here, code, d) for d in range(3)]
        restrict = jnp.concatenate(
            [jnp.where(first_half, parts[0], parts[1]), jnp.where(first_half, parts[2], 0.0)], axis=1
        )
        twice = []
        for side in range(2):
            both = a_ref[i, :, side * 2 * B : (side + 1) * 2 * B]
            turned = pltpu.roll(both, B, 1)
            twice += [jnp.where(first_half, both, turned), jnp.where(first_half, turned, both)]
        result = lax.dot_general(
            restrict, jnp.concatenate(twice, axis=1), (((0,), (0,)), ((), ())),
            precision=lax.Precision.HIGHEST, preferred_element_type=F32,
        )[0 : 3 * B]
        high = result.astype(BF16)
        low = (result - high.astype(F32)).astype(BF16)
        for k in range(KA):
            left_hi[i * KA + k] = high[:, k * 2 * B : (k + 1) * 2 * B]
            left_lo[i * KA + k] = low[:, k * 2 * B : (k + 1) * 2 * B]
        return carry

    wide_half = lax.broadcasted_iota(jnp.int32, (3 * B, 2 * B), 1) < B

    def compute(step):
        for half in range(2):
            row, column = step // 2, 2 * (step % 2) + half
            for slot in range(MB):
                values = got[column, row, slot * B : (slot + 1) * B, :]
                code = jnp.broadcast_to(got[column, row, MB * B + slot : MB * B + slot + 1, :], (B, 2 * B))
                mine = first_half if half == 0 else jnp.logical_not(first_half)
                at_row = (MB * half + slot) * B
                for e in range(3):
                    part = jnp.where(mine, windowed(values, code, e), 0.0)
                    high = part.astype(BF16)
                    win_hi[at_row : at_row + B, e * 2 * B : (e + 1) * 2 * B] = high
                    win_lo[at_row : at_row + B, e * 2 * B : (e + 1) * 2 * B] = (part - high.astype(F32)).astype(BF16)

        def stacked(ref):
            pairs = [ref[pair_tab[2 * MB * step + n]] for n in range(2 * MB)]
            return jnp.concatenate(
                [jnp.where(wide_half, pairs[0], pairs[1]), jnp.where(wide_half, pairs[2], pairs[3])], axis=1
            )

        high, low = stacked(left_hi), stacked(left_lo)
        total = jnp.dot(high, win_hi[...], preferred_element_type=F32)
        total += jnp.dot(high, win_lo[...], preferred_element_type=F32)
        total += jnp.dot(low, win_hi[...], preferred_element_type=F32)
        down_out[step] = total[0:B]
        middle[step] = total[B : 2 * B]
        up_out[step] = total[2 * B : 3 * B]

    def detour(side, turn, n):
        if side == 0:
            return is_last & (n == 1), turn
        return is_first & (turn == 0), n

    def each_way(side, turn, n, act):
        step = 2 * order[turn] + n
        if not far or (side and turn):
            act(halo_copy(step, side))
            return
        around, index = detour(side, turn, n)

        @pl.when(around)
        def _():
            act(pass_copy(side, step, index))

        @pl.when(jnp.logical_not(around))
        def _():
            act(halo_copy(step, side))

    def passed_on(side, turn):
        return [(2 * order[turn] + 1, turn)] if side == 0 else [(2 * order[turn] + n, n) for n in range(2 - 2 * min(turn, 1))]

    def pass_on(side, turn):
        if far:

            @pl.when(is_passer[side])
            def _():
                if side:
                    pl.semaphore_wait(ready.at[4], 1)
                for step, index in passed_on(side, turn):
                    pass_copy(side, step, index).wait_recv()
                    on_copy(side, step, index).start()

    def finish(step):
        halo_copy(step, 0).wait_recv()
        halo_copy(step, 1).wait_recv()
        for e in range(5):
            parts = []
            for ref, shift in ((lower, 0), (middle, 1), (upper, 2)):
                if 0 <= e - shift < 3:
                    parts.append(ref[step, :, (e - shift) * 2 * B : (e - shift + 1) * 2 * B])
            column = pl.multiple_of(e * NX * NY * B + step * 2 * B, 2 * B)
            out_ref[:, pl.ds(column, 2 * B)] = sum(parts[1:], parts[0])

    def both_steps(turn, work):
        def one(n, carry):
            work(2 * order[turn] + n)
            return carry

        lax.fori_loop(0, 2, one, 0)

    def multiply(turn):
        def one(n, carry):
            compute(2 * order[turn] + n)
            for side in range(2):
                each_way(side, turn, n, lambda copy: copy.start())
            return carry

        lax.fori_loop(0, 2, one, 0)

    inputs[4].wait()
    lax.fori_loop(0, 2, left_product, 0)
    for shift in range(1, NX):
        ask_landing(shift).wait_recv()
    serve(0)
    lax.fori_loop(2, 3, left_product, 0)
    y_take(1)
    serve(1)
    lax.fori_loop(3, 4, left_product, 0)
    y_take(2)
    serve(2)

    @pl.when(jnp.logical_not(is_end))
    def _():
        y_take(3)

    if far:

        @pl.when(is_last)
        def _():
            signal(ready.at[2], (blk, below))

    x_take(0)

    @pl.when(jnp.logical_not(is_last))
    def _():
        pl.semaphore_wait(ready.at[0], 1)

    @pl.when(is_first)
    def _():
        pl.semaphore_wait(ready.at[3 if far else 1], 1)

    multiply(0)

    @pl.when(is_end)
    def _():
        y_take(3)

    serve(3)
    x_take(1)
    if far:

        @pl.when(is_first)
        def _():
            pl.semaphore_wait(ready.at[1], 1)

    pass_on(0, 0)
    multiply(1)
    pass_on(1, 0)
    x_take(2)
    pass_on(0, 1)
    multiply(2)
    pass_on(0, 2)
    x_take(3)
    pass_on(0, 3)
    multiply(3)
    for turn in range(4):
        both_steps(turn, finish)

    y_sends(lambda copy: copy.wait_send())

    @pl.when(jnp.logical_not(is_end))
    def _():
        hand_on(0).wait_send()
        hand_on(1).wait_send()

    for shift in range(1, NX):
        ask_copy(shift).wait_send()

    def drain_x(source, carry):
        for shift in range(1, NX):
            x_copy(source, shift).wait_send()
        return carry

    lax.fori_loop(0, NY, drain_x, 0)

    for side in range(2):
        for turn in range(4):
            for n in range(2):
                each_way(side, turn, n, lambda copy: copy.wait_send())
            if far and passed_on(side, turn):

                @pl.when(is_passer[side])
                def _():
                    for step, index in passed_on(side, turn):
                        on_copy(side, step, index).wait_send()


def body(fine_blocks, source_group, source_row, prolong_blocks, prolong_code):
    hbm = pl.BlockSpec(memory_space=pltpu.HBM)
    window = 3 * 2 * B
    halo = pltpu.VMEM((STEPS, B, window), F32)
    dma = pltpu.SemaphoreType.DMA
    return pl.pallas_call(
        kernel,
        out_shape=jax.ShapeDtypeStruct((B, 5 * NX * NY * B), F32),
        in_specs=[hbm] * 5,
        out_specs=pl.BlockSpec(memory_space=pltpu.VMEM),
        scratch_shapes=[
            pltpu.VMEM((FB, B, KA * B), F32),
            pltpu.SMEM((FB, KA), jnp.int32),
            pltpu.SMEM((FB, KA), jnp.int32),
            pltpu.SMEM((2, FB), jnp.int32),
            pltpu.VMEM((NY, PACK, 2 * B), F32),
            pltpu.VMEM((NX, NY * MB, 2 * B), F32),
            pltpu.VMEM((NX, NY * MB, 2 * B), F32),
            pltpu.VMEM((NX, NY, SHARE, 2 * B), F32),
            pltpu.VMEM((NX, NY, SHARE, 2 * B), F32),
            pltpu.VMEM((FB * KA, 3 * B, 2 * B), BF16),
            pltpu.VMEM((FB * KA, 3 * B, 2 * B), BF16),
            pltpu.VMEM((2 * MB * B, window), BF16),
            pltpu.VMEM((2 * MB * B, window), BF16),
            halo, halo, halo, halo, halo,
            pltpu.VMEM((2, max(DETOURS), B, window), F32),
            pltpu.SMEM((MB * NX * NY,), jnp.int32),
            dma((5,)),
            dma((6,)), dma((2, NY)),
            dma((NX,)), dma((NX,)),
            dma((NX, NY)), dma((NX, NY)),
            dma((2, STEPS)), dma((2, STEPS)),
            dma((2, max(DETOURS))), dma((2, max(DETOURS))), dma((2, max(DETOURS))),
            pltpu.SemaphoreType.REGULAR((5,)),
        ],
        compiler_params=pltpu.CompilerParams(
            collective_id=0, has_side_effects=True, vmem_limit_bytes=40 * 2**20
        ),
        cost_estimate=pl.CostEstimate(flops=10**9, bytes_accessed=4 * 2**20, transcendentals=0),
        name="galerkin",
    )(*[
        pltpu.with_memory_space_constraint(each, pltpu.HBM)
        for each in (fine_blocks, prolong_blocks.reshape(FB * B, 2 * B), source_group, source_row, prolong_code.T)
    ])


def solution(mesh):
    return jax.shard_map(
        body,
        mesh=mesh,
        in_specs=(
            P(("blk", "band"), None, None),
            P(("blk", "band"), None),
            P(("blk", "band"), None),
            P(("blk", "band"), None, None),
            P(("blk", "band"), None),
        ),
        out_specs=P(("blk", "band"), None),
        check_vma=False,
    )
```

```python
import jax
import jax.numpy as jnp
from jax import lax
from jax.experimental import pallas as pl
from jax.experimental.pallas import tpu as pltpu
from jax.sharding import PartitionSpec as P

MESH = pl.DeviceIdType.MESH
F32 = jnp.float32
BF16 = jnp.bfloat16

B = 64
FB = 4
KA = 4
MB = 2
NX = 4
NY = 4
PACK = FB * B + 8
SHARE = MB * B + 8
STEPS = NX * NY // 2
DETOURS = (4, 2)
HEAD = 136


def kernel(
    a_hbm, p_hbm, group_hbm, row_hbm, code_hbm, out_ref,
    a_ref, group_ref, row_ref, code_ref,
    held, want, asked, staged, got, left_hi, left_lo, win_hi, win_lo,
    middle, up_out, down_out, lower, upper, passing, pair_tab,
    in_sem, y_send, y_recv, ask_send, ask_recv, x_send, x_recv, halo_send, halo_recv,
    pass_send, pass_recv, on_send, ready,
):
    blk, band = lax.axis_index("blk"), lax.axis_index("band")
    bands = lax.axis_size("band")
    half_bands = bands // 2
    y, x = blk // NX, blk % NX
    above, below = (band + 1) % bands, (band + bands - 1) % bands
    place = band % half_bands
    is_first, is_last = place == 0, place == half_bands - 1
    far = half_bands >= 4
    is_patient, is_passer = place == half_bands - 2, (place == half_bands - 3, place == 2)
    lane = lax.broadcasted_iota(jnp.int32, (B, 2 * B), 1)
    first_half = lane < B

    def at(row, column):
        return (row * NX + column, band)

    def inside(row):
        return (row >= 0) & (row < NY)

    def beside(shift):
        return (x + shift) % NX

    def signal(semaphore, target):
        pl.semaphore_signal(semaphore, inc=1, device_id=target, device_id_type=MESH)

    inputs = [
        pltpu.make_async_copy(source, target, in_sem.at[n])
        for n, (source, target) in enumerate((
            (group_hbm, group_ref), (row_hbm, row_ref), (code_hbm, code_ref),
            (p_hbm, held.at[y, pl.ds(0, FB * B)]), (a_hbm, a_ref),
        ))
    ]
    for copy in inputs:
        copy.start()

    barrier = pltpu.get_barrier_semaphore()
    for shift in range(1, NX):
        signal(barrier, at(y, beside(shift)))

    for jump in (1, -1, 2, -2):

        @pl.when(inside(y + jump))
        def _():
            signal(barrier, at(y + jump, x))

    @pl.when(jnp.logical_not(is_last))
    def _():
        signal(barrier, (blk, above))

    @pl.when(is_first)
    def _():
        signal(barrier, (blk, below))
        if far:
            signal(barrier, (blk, (band + bands - 3) % bands))
            signal(barrier, (blk, band + 2))

    if far:

        @pl.when(is_passer[0])
        def _():
            signal(barrier, (blk, band + 2))

        @pl.when(is_passer[1])
        def _():
            signal(barrier, (blk, (band + bands - 3) % bands))

    inputs[2].wait()
    tile_row = lax.broadcasted_iota(jnp.int32, (8, 2 * B), 0)
    tile_lane = lax.broadcasted_iota(jnp.int32, (8, 2 * B), 1)
    codes = jnp.zeros((8, 2 * B), F32)
    for i in range(FB):
        one = jnp.where(tile_lane < B, code_ref[0, i], code_ref[1, i]).astype(F32)
        codes = jnp.where(tile_row == i, one, codes)
    held[y, FB * B : PACK, :] = codes
    inputs[3].wait()

    pl.semaphore_wait(
        barrier,
        NX - 1 + sum(jnp.where(inside(y + jump), 1, 0) for jump in (1, -1, 2, -2))
        + jnp.where(is_first, 0, 1) + jnp.where(is_last, 3 if far else 1, 0)
        + (jnp.where(is_passer[0] | is_passer[1], 1, 0) if far else 0),
    )

    def y_copy(source, target, sender, part=None):
        rows = pl.ds(0, PACK) if part is None else (pl.ds(0, HEAD), pl.ds(HEAD, PACK - HEAD))[part]
        slot = held.at[source, rows]
        return pltpu.make_async_remote_copy(
            src_ref=slot, dst_ref=slot, send_sem=y_send.at[sender], recv_sem=y_recv.at[part or 0, source],
            device_id=at(target, x), device_id_type=MESH,
        )

    def ask_copy(shift):
        return pltpu.make_async_remote_copy(
            src_ref=want.at[beside(shift)], dst_ref=asked.at[NX - shift],
            send_sem=ask_send.at[shift], recv_sem=ask_recv.at[NX - shift],
            device_id=at(y, beside(shift)), device_id_type=MESH,
        )

    def x_copy(source, shift):
        return pltpu.make_async_remote_copy(
            src_ref=staged.at[shift, source], dst_ref=got.at[x, source],
            send_sem=x_send.at[shift, source], recv_sem=x_recv.at[shift, source],
            device_id=at(y, beside(shift)), device_id_type=MESH,
        )

    def x_landing(source, shift):
        return pltpu.make_async_remote_copy(
            src_ref=staged.at[shift, source], dst_ref=got.at[beside(NX - shift), source],
            send_sem=x_send.at[shift, source], recv_sem=x_recv.at[shift, source],
            device_id=at(y, beside(shift)), device_id_type=MESH,
        )

    def ask_landing(shift):
        return pltpu.make_async_remote_copy(
            src_ref=want.at[beside(shift)], dst_ref=asked.at[shift],
            send_sem=ask_send.at[shift], recv_sem=ask_recv.at[shift],
            device_id=at(y, beside(shift)), device_id_type=MESH,
        )

    def halo_copy(step, side):
        return pltpu.make_async_remote_copy(
            src_ref=(down_out if side else up_out).at[step], dst_ref=(upper if side else lower).at[step],
            send_sem=halo_send.at[side, step], recv_sem=halo_recv.at[side, step],
            device_id=(blk, below if side else above), device_id_type=MESH,
        )

    def pass_copy(side, step, n):
        return pltpu.make_async_remote_copy(
            src_ref=(down_out if side else up_out).at[step], dst_ref=passing.at[side, n],
            send_sem=pass_send.at[side, n], recv_sem=pass_recv.at[side, n],
            device_id=(blk, (band + (2 if side else bands - 2)) % bands), device_id_type=MESH,
        )

    def on_copy(side, step, n):
        return pltpu.make_async_remote_copy(
            src_ref=passing.at[side, n], dst_ref=(upper if side else lower).at[step],
            send_sem=on_send.at[side, n], recv_sem=halo_recv.at[side, step],
            device_id=(blk, (band + (bands - 3 if side else 3)) % bands), device_id_type=MESH,
        )

    order = [
        y,
        jnp.where(y == 0, 1, y - 1),
        jnp.where(y == 0, 2, jnp.where(y == 3, 1, y + 1)),
        jnp.where(y < 2, 3, 0),
    ]

    is_end = (y == 0) | (y == NY - 1)
    end_jump = jnp.where(y == 0, 1, -1)
    inner_jump = jnp.where(y == 1, 1, -1)
    hand_source, hand_target = jnp.where(y == 1, 3, 0), jnp.where(y == 1, 0, 3)

    def y_sends(act):
        @pl.when(is_end)
        def _():
            act(y_copy(y, y + 2 * end_jump, 0, 0))
            act(y_copy(y, y + 2 * end_jump, 1, 1))
            act(y_copy(y, y + end_jump, 2))

        @pl.when(jnp.logical_not(is_end))
        def _():
            act(y_copy(y, y + inner_jump, 2))
            act(y_copy(y, y - inner_jump, 3))
            act(y_copy(y, y + 2 * inner_jump, 0))

    def hand_on(part):
        return y_copy(hand_source, hand_target, 4 + part, part)

    def serve(turn):
        source = order[turn]

        def choose(wanted, slot, target):
            row = wanted(MB * source + slot)
            pick = jnp.broadcast_to(row, (B, 2 * B))
            values = jnp.zeros((B, 2 * B), F32)
            code = jnp.zeros((1, 2 * B), F32)
            for i in range(FB):
                values = jnp.where(pick == i, held[source, i * B : (i + 1) * B, :], values)
                code = jnp.where(row == i, held[source, FB * B + i : FB * B + i + 1, :], code)
            target(slice(slot * B, (slot + 1) * B), values)
            target(slice(MB * B + slot, MB * B + slot + 1), code)

        for shift in (2, 1, 3):
            for slot in range(MB):

                def wanted(n, shift=shift):
                    return asked[shift, pl.ds(n, 1), :]

                def target(rows, values, shift=shift):
                    staged[shift, source, rows, :] = values

                choose(wanted, slot, target)
            x_copy(source, shift).start()
        for slot in range(MB):

            def own(n):
                return want[x, pl.ds(n, 1), :]

            def keep(rows, values):
                got[x, source, rows, :] = values

            choose(own, slot, keep)

    def y_take(turn):
        source = order[turn]
        sender = jnp.where(source < y, y - 1, y + 1)
        if turn < 3:
            y_copy(source, sender, 0).wait_recv()
            return
        for part in range(2):
            y_copy(source, sender, 0, part).wait_recv()

            @pl.when(jnp.logical_not(is_end))
            def _():
                hand_on(part).start()

    def x_take(turn):
        for shift in range(1, NX):
            x_landing(order[turn], shift).wait_recv()

    @pl.when(jnp.logical_not(is_first))
    def _():
        signal(ready.at[0], (blk, below))

    @pl.when(is_last)
    def _():
        signal(ready.at[1], (blk, above))
        if far:
            signal(ready.at[4], (blk, (band + 3) % bands))

    if far:

        @pl.when(is_passer[1])
        def _():
            signal(ready.at[3], (blk, band - 2))

        @pl.when(is_patient)
        def _():
            pl.semaphore_wait(ready.at[2], 1)

    y_sends(lambda copy: copy.start())

    for copy in inputs[0:2]:
        copy.wait()

    def tabulate(group, carry):
        pair = [jnp.int32(0), jnp.int32(0)]
        row = [jnp.int32(FB), jnp.int32(FB)]
        for at_pair in range(FB * KA - 1, -1, -1):
            i, k = at_pair // KA, at_pair % KA
            hit = group_ref[i, k] == group
            pair = [jnp.where(hit, at_pair, pair[0]), jnp.where(hit, pair[0], pair[1])]
            row = [jnp.where(hit, row_ref[i, k], row[0]), jnp.where(hit, row[0], row[1])]
        for slot in range(MB):
            pair_tab[MB * group + slot] = pair[slot]
            want[group % NX, pl.ds(MB * (group // NX) + slot, 1), :] = jnp.full((1, 2 * B), row[slot]).astype(F32)
        return carry

    lax.fori_loop(0, NX * NY, tabulate, 0)

    for shift in (2, 1, 3):
        ask_copy(shift).start()

    def windowed(values, code, at_code):
        chosen = jnp.where(code == at_code, values, 0.0)
        return chosen + pltpu.roll(chosen, B, 1)

    def left_product(i, carry):
        p_here = held[y, pl.ds(pl.multiple_of(i * B, B), B), :]
        code = jnp.broadcast_to(held[y, pl.ds(FB * B + i, 1), :], (B, 2 * B))
        parts = [windowed(p_here, code, d) for d in range(3)]
        restrict = jnp.concatenate(
            [jnp.where(first_half, parts[0], parts[1]), jnp.where(first_half, parts[2], 0.0)], axis=1
        )
        twice = []
        for side in range(2):
            both = a_ref[i, :, side * 2 * B : (side + 1) * 2 * B]
            turned = pltpu.roll(both, B, 1)
            twice += [jnp.where(first_half, both, turned), jnp.where(first_half, turned, both)]
        result = lax.dot_general(
            restrict, jnp.concatenate(twice, axis=1), (((0,), (0,)), ((), ())),
            precision=lax.Precision.HIGHEST, preferred_element_type=F32,
        )[0 : 3 * B]
        high = result.astype(BF16)
        low = (result - high.astype(F32)).astype(BF16)
        for k in range(KA):
            left_hi[i * KA + k] = high[:, k * 2 * B : (k + 1) * 2 * B]
            left_lo[i * KA + k] = low[:, k * 2 * B : (k + 1) * 2 * B]
        return carry

    wide_half = lax.broadcasted_iota(jnp.int32, (3 * B, 2 * B), 1) < B

    def compute(step):
        for half in range(2):
            row, column = step // 2, 2 * (step % 2) + half
            for slot in range(MB):
                values = got[column, row, slot * B : (slot + 1) * B, :]
                code = jnp.broadcast_to(got[column, row, MB * B + slot : MB * B + slot + 1, :], (B, 2 * B))
                mine = first_half if half == 0 else jnp.logical_not(first_half)
                at_row = (MB * half + slot) * B
                for e in range(3):
                    part = jnp.where(mine, windowed(values, code, e), 0.0)
                    high = part.astype(BF16)
                    win_hi[at_row : at_row + B, e * 2 * B : (e + 1) * 2 * B] = high
                    win_lo[at_row : at_row + B, e * 2 * B : (e + 1) * 2 * B] = (part - high.astype(F32)).astype(BF16)

        def stacked(ref):
            pairs = [ref[pair_tab[2 * MB * step + n]] for n in range(2 * MB)]
            return jnp.concatenate(
                [jnp.where(wide_half, pairs[0], pairs[1]), jnp.where(wide_half, pairs[2], pairs[3])], axis=1
            )

        high, low = stacked(left_hi), stacked(left_lo)
        total = jnp.dot(high, win_hi[...], preferred_element_type=F32)
        total += jnp.dot(high, win_lo[...], preferred_element_type=F32)
        total += jnp.dot(low, win_hi[...], preferred_element_type=F32)
        down_out[step] = total[0:B]
        middle[step] = total[B : 2 * B]
        up_out[step] = total[2 * B : 3 * B]

    def detour(side, turn, n):
        if side == 0:
            return is_last & (n == 0), turn
        return is_first & (turn == 0), n

    def each_way(side, turn, n, act):
        step = 2 * order[turn] + n
        if not far or (side and turn):
            act(halo_copy(step, side))
            return
        around, index = detour(side, turn, n)

        @pl.when(around)
        def _():
            act(pass_copy(side, step, index))

        @pl.when(jnp.logical_not(around))
        def _():
            act(halo_copy(step, side))

    def passed_on(side, turn):
        return [(2 * order[turn], turn)] if side == 0 else [(2 * order[turn] + n, n) for n in range(2 - 2 * min(turn, 1))]

    def pass_on(side, turn):
        if far:

            @pl.when(is_passer[side])
            def _():
                if side:
                    pl.semaphore_wait(ready.at[4], 1)
                for step, index in passed_on(side, turn):
                    pass_copy(side, step, index).wait_recv()
                    on_copy(side, step, index).start()

    def finish(step):
        halo_copy(step, 0).wait_recv()
        halo_copy(step, 1).wait_recv()
        for e in range(5):
            parts = []
            for ref, shift in ((lower, 0), (middle, 1), (upper, 2)):
                if 0 <= e - shift < 3:
                    parts.append(ref[step, :, (e - shift) * 2 * B : (e - shift + 1) * 2 * B])
            column = pl.multiple_of(e * NX * NY * B + step * 2 * B, 2 * B)
            out_ref[:, pl.ds(column, 2 * B)] = sum(parts[1:], parts[0])

    def both_steps(turn, work):
        def one(n, carry):
            work(2 * order[turn] + n)
            return carry

        lax.fori_loop(0, 2, one, 0)

    def multiply(turn):
        def one(n, carry):
            compute(2 * order[turn] + n)
            for side in range(2):
                each_way(side, turn, n, lambda copy: copy.start())
            return carry

        lax.fori_loop(0, 2, one, 0)

    inputs[4].wait()
    lax.fori_loop(0, 2, left_product, 0)
    for shift in range(1, NX):
        ask_landing(shift).wait_recv()
    serve(0)
    lax.fori_loop(2, 3, left_product, 0)
    y_take(1)
    serve(1)
    lax.fori_loop(3, 4, left_product, 0)
    y_take(2)
    serve(2)

    @pl.when(jnp.logical_not(is_end))
    def _():
        y_take(3)

    if far:

        @pl.when(is_last)
        def _():
            signal(ready.at[2], (blk, below))

    x_take(0)

    @pl.when(jnp.logical_not(is_last))
    def _():
        pl.semaphore_wait(ready.at[0], 1)

    @pl.when(is_first)
    def _():
        pl.semaphore_wait(ready.at[3 if far else 1], 1)

    multiply(0)

    @pl.when(is_end)
    def _():
        y_take(3)

    serve(3)
    x_take(1)
    if far:

        @pl.when(is_first)
        def _():
            pl.semaphore_wait(ready.at[1], 1)

    pass_on(0, 0)
    multiply(1)
    pass_on(1, 0)
    x_take(2)
    pass_on(0, 1)
    multiply(2)
    pass_on(0, 2)
    pass_on(0, 3)
    x_take(3)
    multiply(3)
    for turn in range(4):
        both_steps(turn, finish)

    y_sends(lambda copy: copy.wait_send())

    @pl.when(jnp.logical_not(is_end))
    def _():
        hand_on(0).wait_send()
        hand_on(1).wait_send()

    for shift in range(1, NX):
        ask_copy(shift).wait_send()

    def drain_x(source, carry):
        for shift in range(1, NX):
            x_copy(source, shift).wait_send()
        return carry

    lax.fori_loop(0, NY, drain_x, 0)

    for side in range(2):
        for turn in range(4):
            for n in range(2):
                each_way(side, turn, n, lambda copy: copy.wait_send())
            if far and passed_on(side, turn):

                @pl.when(is_passer[side])
                def _():
                    for step, index in passed_on(side, turn):
                        on_copy(side, step, index).wait_send()


def body(fine_blocks, source_group, source_row, prolong_blocks, prolong_code):
    hbm = pl.BlockSpec(memory_space=pltpu.HBM)
    window = 3 * 2 * B
    halo = pltpu.VMEM((STEPS, B, window), F32)
    dma = pltpu.SemaphoreType.DMA
    return pl.pallas_call(
        kernel,
        out_shape=jax.ShapeDtypeStruct((B, 5 * NX * NY * B), F32),
        in_specs=[hbm] * 5,
        out_specs=pl.BlockSpec(memory_space=pltpu.VMEM),
        scratch_shapes=[
            pltpu.VMEM((FB, B, KA * B), F32),
            pltpu.SMEM((FB, KA), jnp.int32),
            pltpu.SMEM((FB, KA), jnp.int32),
            pltpu.SMEM((2, FB), jnp.int32),
            pltpu.VMEM((NY, PACK, 2 * B), F32),
            pltpu.VMEM((NX, NY * MB, 2 * B), F32),
            pltpu.VMEM((NX, NY * MB, 2 * B), F32),
            pltpu.VMEM((NX, NY, SHARE, 2 * B), F32),
            pltpu.VMEM((NX, NY, SHARE, 2 * B), F32),
            pltpu.VMEM((FB * KA, 3 * B, 2 * B), BF16),
            pltpu.VMEM((FB * KA, 3 * B, 2 * B), BF16),
            pltpu.VMEM((2 * MB * B, window), BF16),
            pltpu.VMEM((2 * MB * B, window), BF16),
            halo, halo, halo, halo, halo,
            pltpu.VMEM((2, max(DETOURS), B, window), F32),
            pltpu.SMEM((MB * NX * NY,), jnp.int32),
            dma((5,)),
            dma((6,)), dma((2, NY)),
            dma((NX,)), dma((NX,)),
            dma((NX, NY)), dma((NX, NY)),
            dma((2, STEPS)), dma((2, STEPS)),
            dma((2, max(DETOURS))), dma((2, max(DETOURS))), dma((2, max(DETOURS))),
            pltpu.SemaphoreType.REGULAR((5,)),
        ],
        compiler_params=pltpu.CompilerParams(
            collective_id=0, has_side_effects=True, vmem_limit_bytes=40 * 2**20
        ),
        cost_estimate=pl.CostEstimate(flops=10**9, bytes_accessed=4 * 2**20, transcendentals=0),
        name="galerkin",
    )(*[
        pltpu.with_memory_space_constraint(each, pltpu.HBM)
        for each in (fine_blocks, prolong_blocks.reshape(FB * B, 2 * B), source_group, source_row, prolong_code.T)
    ])


def solution(mesh):
    return jax.shard_map(
        body,
        mesh=mesh,
        in_specs=(
            P(("blk", "band"), None, None),
            P(("blk", "band"), None),
            P(("blk", "band"), None),
            P(("blk", "band"), None, None),
            P(("blk", "band"), None),
        ),
        out_specs=P(("blk", "band"), None),
        check_vma=False,
    )
```

```python
import jax
import jax.numpy as jnp
from jax import lax
from jax.experimental import pallas as pl
from jax.experimental.pallas import tpu as pltpu
from jax.sharding import PartitionSpec as P

MESH = pl.DeviceIdType.MESH
F32 = jnp.float32
BF16 = jnp.bfloat16

B = 64
FB = 4
KA = 4
MB = 2
NX = 4
NY = 4
PACK = FB * B + 8
SHARE = MB * B + 8
STEPS = NX * NY // 2
DETOURS = (4, 2)
HEAD = 136


def kernel(
    a_hbm, p_hbm, group_hbm, row_hbm, code_hbm, out_ref,
    a_ref, group_ref, row_ref, code_ref,
    held, want, asked, staged, got, left_hi, left_lo, win_hi, win_lo,
    middle, up_out, down_out, lower, upper, passing, pair_tab,
    in_sem, y_send, y_recv, ask_send, ask_recv, x_send, x_recv, halo_send, halo_recv,
    pass_send, pass_recv, on_send, ready,
):
    blk, band = lax.axis_index("blk"), lax.axis_index("band")
    bands = lax.axis_size("band")
    half_bands = bands // 2
    y, x = blk // NX, blk % NX
    above, below = (band + 1) % bands, (band + bands - 1) % bands
    place = band % half_bands
    is_first, is_last = place == 0, place == half_bands - 1
    far = half_bands >= 4
    is_patient, is_passer = place == half_bands - 2, (place == half_bands - 3, place == 2)
    lane = lax.broadcasted_iota(jnp.int32, (B, 2 * B), 1)
    first_half = lane < B

    def at(row, column):
        return (row * NX + column, band)

    def inside(row):
        return (row >= 0) & (row < NY)

    def beside(shift):
        return (x + shift) % NX

    def signal(semaphore, target):
        pl.semaphore_signal(semaphore, inc=1, device_id=target, device_id_type=MESH)

    inputs = [
        pltpu.make_async_copy(source, target, in_sem.at[n])
        for n, (source, target) in enumerate((
            (group_hbm, group_ref), (row_hbm, row_ref), (code_hbm, code_ref),
            (p_hbm, held.at[y, pl.ds(0, FB * B)]), (a_hbm, a_ref),
        ))
    ]
    for copy in inputs:
        copy.start()

    barrier = pltpu.get_barrier_semaphore()
    for shift in range(1, NX):
        signal(barrier, at(y, beside(shift)))

    for jump in (1, -1, 2, -2):

        @pl.when(inside(y + jump))
        def _():
            signal(barrier, at(y + jump, x))

    @pl.when(jnp.logical_not(is_last))
    def _():
        signal(barrier, (blk, above))

    @pl.when(is_first)
    def _():
        signal(barrier, (blk, below))
        if far:
            signal(barrier, (blk, (band + bands - 3) % bands))
            signal(barrier, (blk, band + 2))

    if far:

        @pl.when(is_passer[0])
        def _():
            signal(barrier, (blk, band + 2))

        @pl.when(is_passer[1])
        def _():
            signal(barrier, (blk, (band + bands - 3) % bands))

    inputs[2].wait()
    tile_row = lax.broadcasted_iota(jnp.int32, (8, 2 * B), 0)
    tile_lane = lax.broadcasted_iota(jnp.int32, (8, 2 * B), 1)
    codes = jnp.zeros((8, 2 * B), F32)
    for i in range(FB):
        one = jnp.where(tile_lane < B, code_ref[0, i], code_ref[1, i]).astype(F32)
        codes = jnp.where(tile_row == i, one, codes)
    held[y, FB * B : PACK, :] = codes
    inputs[3].wait()

    pl.semaphore_wait(
        barrier,
        NX - 1 + sum(jnp.where(inside(y + jump), 1, 0) for jump in (1, -1, 2, -2))
        + jnp.where(is_first, 0, 1) + jnp.where(is_last, 3 if far else 1, 0)
        + (jnp.where(is_passer[0] | is_passer[1], 1, 0) if far else 0),
    )

    def y_copy(source, target, sender, part=None):
        rows = pl.ds(0, PACK) if part is None else (pl.ds(0, HEAD), pl.ds(HEAD, PACK - HEAD))[part]
        slot = held.at[source, rows]
        return pltpu.make_async_remote_copy(
            src_ref=slot, dst_ref=slot, send_sem=y_send.at[sender], recv_sem=y_recv.at[part or 0, source],
            device_id=at(target, x), device_id_type=MESH,
        )

    def ask_copy(shift):
        return pltpu.make_async_remote_copy(
            src_ref=want.at[beside(shift)], dst_ref=asked.at[NX - shift],
            send_sem=ask_send.at[shift], recv_sem=ask_recv.at[NX - shift],
            device_id=at(y, beside(shift)), device_id_type=MESH,
        )

    def x_copy(source, shift):
        return pltpu.make_async_remote_copy(
            src_ref=staged.at[shift, source], dst_ref=got.at[x, source],
            send_sem=x_send.at[shift, source], recv_sem=x_recv.at[shift, source],
            device_id=at(y, beside(shift)), device_id_type=MESH,
        )

    def x_landing(source, shift):
        return pltpu.make_async_remote_copy(
            src_ref=staged.at[shift, source], dst_ref=got.at[beside(NX - shift), source],
            send_sem=x_send.at[shift, source], recv_sem=x_recv.at[shift, source],
            device_id=at(y, beside(shift)), device_id_type=MESH,
        )

    def ask_landing(shift):
        return pltpu.make_async_remote_copy(
            src_ref=want.at[beside(shift)], dst_ref=asked.at[shift],
            send_sem=ask_send.at[shift], recv_sem=ask_recv.at[shift],
            device_id=at(y, beside(shift)), device_id_type=MESH,
        )

    def halo_copy(step, side):
        return pltpu.make_async_remote_copy(
            src_ref=(down_out if side else up_out).at[step], dst_ref=(upper if side else lower).at[step],
            send_sem=halo_send.at[side, step], recv_sem=halo_recv.at[side, step],
            device_id=(blk, below if side else above), device_id_type=MESH,
        )

    def pass_copy(side, step, n):
        return pltpu.make_async_remote_copy(
            src_ref=(down_out if side else up_out).at[step], dst_ref=passing.at[side, n],
            send_sem=pass_send.at[side, n], recv_sem=pass_recv.at[side, n],
            device_id=(blk, (band + (2 if side else bands - 2)) % bands), device_id_type=MESH,
        )

    def on_copy(side, step, n):
        return pltpu.make_async_remote_copy(
            src_ref=passing.at[side, n], dst_ref=(upper if side else lower).at[step],
            send_sem=on_send.at[side, n], recv_sem=halo_recv.at[side, step],
            device_id=(blk, (band + (bands - 3 if side else 3)) % bands), device_id_type=MESH,
        )

    order = [
        y,
        jnp.where(y == 0, 1, y - 1),
        jnp.where(y == 0, 2, jnp.where(y == 3, 1, y + 1)),
        jnp.where(y < 2, 3, 0),
    ]

    is_end = (y == 0) | (y == NY - 1)
    end_jump = jnp.where(y == 0, 1, -1)
    inner_jump = jnp.where(y == 1, 1, -1)
    hand_source, hand_target = jnp.where(y == 1, 3, 0), jnp.where(y == 1, 0, 3)

    def y_sends(act):
        @pl.when(is_end)
        def _():
            act(y_copy(y, y + 2 * end_jump, 0, 0))
            act(y_copy(y, y + 2 * end_jump, 1, 1))
            act(y_copy(y, y + end_jump, 2))

        @pl.when(jnp.logical_not(is_end))
        def _():
            act(y_copy(y, y + inner_jump, 2))
            act(y_copy(y, y - inner_jump, 3))
            act(y_copy(y, y + 2 * inner_jump, 0))

    def hand_on(part):
        return y_copy(hand_source, hand_target, 4 + part, part)

    def serve(turn):
        source = order[turn]

        def choose(wanted, slot, target):
            row = wanted(MB * source + slot)
            pick = jnp.broadcast_to(row, (B, 2 * B))
            values = jnp.zeros((B, 2 * B), F32)
            code = jnp.zeros((1, 2 * B), F32)
            for i in range(FB):
                values = jnp.where(pick == i, held[source, i * B : (i + 1) * B, :], values)
                code = jnp.where(row == i, held[source, FB * B + i : FB * B + i + 1, :], code)
            target(slice(slot * B, (slot + 1) * B), values)
            target(slice(MB * B + slot, MB * B + slot + 1), code)

        for shift in (2, 1, 3):
            for slot in range(MB):

                def wanted(n, shift=shift):
                    return asked[shift, pl.ds(n, 1), :]

                def target(rows, values, shift=shift):
                    staged[shift, source, rows, :] = values

                choose(wanted, slot, target)
            x_copy(source, shift).start()
        for slot in range(MB):

            def own(n):
                return want[x, pl.ds(n, 1), :]

            def keep(rows, values):
                got[x, source, rows, :] = values

            choose(own, slot, keep)

    def y_take(turn):
        source = order[turn]
        sender = jnp.where(source < y, y - 1, y + 1)
        if turn < 3:
            y_copy(source, sender, 0).wait_recv()
            return
        for part in range(2):
            y_copy(source, sender, 0, part).wait_recv()

            @pl.when(jnp.logical_not(is_end))
            def _():
                hand_on(part).start()

    def x_take(turn):
        for shift in range(1, NX):
            x_landing(order[turn], shift).wait_recv()

    @pl.when(jnp.logical_not(is_first))
    def _():
        signal(ready.at[0], (blk, below))

    @pl.when(is_last)
    def _():
        signal(ready.at[1], (blk, above))
        if far:
            signal(ready.at[4], (blk, (band + 3) % bands))

    if far:

        @pl.when(is_passer[1])
        def _():
            signal(ready.at[3], (blk, band - 2))

        @pl.when(is_patient)
        def _():
            pl.semaphore_wait(ready.at[2], 1)

    y_sends(lambda copy: copy.start())

    for copy in inputs[0:2]:
        copy.wait()

    def tabulate(group, carry):
        pair = [jnp.int32(0), jnp.int32(0)]
        row = [jnp.int32(FB), jnp.int32(FB)]
        for at_pair in range(FB * KA - 1, -1, -1):
            i, k = at_pair // KA, at_pair % KA
            hit = group_ref[i, k] == group
            pair = [jnp.where(hit, at_pair, pair[0]), jnp.where(hit, pair[0], pair[1])]
            row = [jnp.where(hit, row_ref[i, k], row[0]), jnp.where(hit, row[0], row[1])]
        for slot in range(MB):
            pair_tab[MB * group + slot] = pair[slot]
            want[group % NX, pl.ds(MB * (group // NX) + slot, 1), :] = jnp.full((1, 2 * B), row[slot]).astype(F32)
        return carry

    lax.fori_loop(0, NX * NY, tabulate, 0)

    for shift in (2, 1, 3):
        ask_copy(shift).start()

    def windowed(values, code, at_code):
        chosen = jnp.where(code == at_code, values, 0.0)
        return chosen + pltpu.roll(chosen, B, 1)

    def left_product(i, carry):
        p_here = held[y, pl.ds(pl.multiple_of(i * B, B), B), :]
        code = jnp.broadcast_to(held[y, pl.ds(FB * B + i, 1), :], (B, 2 * B))
        parts = [windowed(p_here, code, d) for d in range(3)]
        restrict = jnp.concatenate(
            [jnp.where(first_half, parts[0], parts[1]), jnp.where(first_half, parts[2], 0.0)], axis=1
        )
        twice = []
        for side in range(2):
            both = a_ref[i, :, side * 2 * B : (side + 1) * 2 * B]
            turned = pltpu.roll(both, B, 1)
            twice += [jnp.where(first_half, both, turned), jnp.where(first_half, turned, both)]
        result = lax.dot_general(
            restrict, jnp.concatenate(twice, axis=1), (((0,), (0,)), ((), ())),
            precision=lax.Precision.HIGHEST, preferred_element_type=F32,
        )[0 : 3 * B]
        high = result.astype(BF16)
        low = (result - high.astype(F32)).astype(BF16)
        for k in range(KA):
            left_hi[i * KA + k] = high[:, k * 2 * B : (k + 1) * 2 * B]
            left_lo[i * KA + k] = low[:, k * 2 * B : (k + 1) * 2 * B]
        return carry

    wide_half = lax.broadcasted_iota(jnp.int32, (3 * B, 2 * B), 1) < B

    def compute(step):
        for half in range(2):
            row, column = step // 2, 2 * (step % 2) + half
            for slot in range(MB):
                values = got[column, row, slot * B : (slot + 1) * B, :]
                code = jnp.broadcast_to(got[column, row, MB * B + slot : MB * B + slot + 1, :], (B, 2 * B))
                mine = first_half if half == 0 else jnp.logical_not(first_half)
                at_row = (MB * half + slot) * B
                for e in range(3):
                    part = jnp.where(mine, windowed(values, code, e), 0.0)
                    high = part.astype(BF16)
                    win_hi[at_row : at_row + B, e * 2 * B : (e + 1) * 2 * B] = high
                    win_lo[at_row : at_row + B, e * 2 * B : (e + 1) * 2 * B] = (part - high.astype(F32)).astype(BF16)

        def stacked(ref):
            pairs = [ref[pair_tab[2 * MB * step + n]] for n in range(2 * MB)]
            return jnp.concatenate(
                [jnp.where(wide_half, pairs[0], pairs[1]), jnp.where(wide_half, pairs[2], pairs[3])], axis=1
            )

        high, low = stacked(left_hi), stacked(left_lo)
        total = jnp.dot(high, win_hi[...], preferred_element_type=F32)
        total += jnp.dot(high, win_lo[...], preferred_element_type=F32)
        total += jnp.dot(low, win_hi[...], preferred_element_type=F32)
        down_out[step] = total[0:B]
        middle[step] = total[B : 2 * B]
        up_out[step] = total[2 * B : 3 * B]

    def detour(side, turn, n):
        if side == 0:
            return is_last & (n == 0), turn
        return is_first & (turn == 0), n

    def each_way(side, turn, n, act):
        step = 2 * order[turn] + n
        if not far or (side and turn):
            act(halo_copy(step, side))
            return
        around, index = detour(side, turn, n)

        @pl.when(around)
        def _():
            act(pass_copy(side, step, index))

        @pl.when(jnp.logical_not(around))
        def _():
            act(halo_copy(step, side))

    def passed_on(side, turn):
        return [(2 * order[turn], turn)] if side == 0 else [(2 * order[turn] + n, n) for n in range(2 - 2 * min(turn, 1))]

    def pass_on(side, turn):
        if far:

            @pl.when(is_passer[side])
            def _():
                if side:
                    pl.semaphore_wait(ready.at[4], 1)
                for step, index in passed_on(side, turn):
                    pass_copy(side, step, index).wait_recv()
                    on_copy(side, step, index).start()

    def finish(step):
        halo_copy(step, 0).wait_recv()
        halo_copy(step, 1).wait_recv()
        for e in range(5):
            parts = []
            for ref, shift in ((lower, 0), (middle, 1), (upper, 2)):
                if 0 <= e - shift < 3:
                    parts.append(ref[step, :, (e - shift) * 2 * B : (e - shift + 1) * 2 * B])
            column = pl.multiple_of(e * NX * NY * B + step * 2 * B, 2 * B)
            out_ref[:, pl.ds(column, 2 * B)] = sum(parts[1:], parts[0])

    def both_steps(turn, work):
        def one(n, carry):
            work(2 * order[turn] + n)
            return carry

        lax.fori_loop(0, 2, one, 0)

    def multiply(turn):
        def one(n, carry):
            compute(2 * order[turn] + n)
            for side in range(2):
                each_way(side, turn, n, lambda copy: copy.start())
            return carry

        lax.fori_loop(0, 2, one, 0)

    inputs[4].wait()
    lax.fori_loop(0, 2, left_product, 0)
    for shift in range(1, NX):
        ask_landing(shift).wait_recv()
    serve(0)
    y_take(1)
    serve(1)
    y_take(2)
    serve(2)

    @pl.when(jnp.logical_not(is_end))
    def _():
        y_take(3)

    if far:

        @pl.when(is_last)
        def _():
            signal(ready.at[2], (blk, below))

    lax.fori_loop(2, FB, left_product, 0)
    x_take(0)

    @pl.when(jnp.logical_not(is_last))
    def _():
        pl.semaphore_wait(ready.at[0], 1)

    @pl.when(is_first)
    def _():
        pl.semaphore_wait(ready.at[3 if far else 1], 1)

    multiply(0)

    @pl.when(is_end)
    def _():
        y_take(3)

    serve(3)
    x_take(1)
    if far:

        @pl.when(is_first)
        def _():
            pl.semaphore_wait(ready.at[1], 1)

    pass_on(0, 0)
    multiply(1)
    pass_on(1, 0)
    x_take(2)
    pass_on(0, 1)
    multiply(2)
    pass_on(0, 2)
    pass_on(0, 3)
    x_take(3)
    multiply(3)
    for turn in range(4):
        both_steps(turn, finish)

    y_sends(lambda copy: copy.wait_send())

    @pl.when(jnp.logical_not(is_end))
    def _():
        hand_on(0).wait_send()
        hand_on(1).wait_send()

    for shift in range(1, NX):
        ask_copy(shift).wait_send()

    def drain_x(source, carry):
        for shift in range(1, NX):
            x_copy(source, shift).wait_send()
        return carry

    lax.fori_loop(0, NY, drain_x, 0)

    for side in range(2):
        for turn in range(4):
            for n in range(2):
                each_way(side, turn, n, lambda copy: copy.wait_send())
            if far and passed_on(side, turn):

                @pl.when(is_passer[side])
                def _():
                    for step, index in passed_on(side, turn):
                        on_copy(side, step, index).wait_send()


def body(fine_blocks, source_group, source_row, prolong_blocks, prolong_code):
    hbm = pl.BlockSpec(memory_space=pltpu.HBM)
    window = 3 * 2 * B
    halo = pltpu.VMEM((STEPS, B, window), F32)
    dma = pltpu.SemaphoreType.DMA
    return pl.pallas_call(
        kernel,
        out_shape=jax.ShapeDtypeStruct((B, 5 * NX * NY * B), F32),
        in_specs=[hbm] * 5,
        out_specs=pl.BlockSpec(memory_space=pltpu.VMEM),
        scratch_shapes=[
            pltpu.VMEM((FB, B, KA * B), F32),
            pltpu.SMEM((FB, KA), jnp.int32),
            pltpu.SMEM((FB, KA), jnp.int32),
            pltpu.SMEM((2, FB), jnp.int32),
            pltpu.VMEM((NY, PACK, 2 * B), F32),
            pltpu.VMEM((NX, NY * MB, 2 * B), F32),
            pltpu.VMEM((NX, NY * MB, 2 * B), F32),
            pltpu.VMEM((NX, NY, SHARE, 2 * B), F32),
            pltpu.VMEM((NX, NY, SHARE, 2 * B), F32),
            pltpu.VMEM((FB * KA, 3 * B, 2 * B), BF16),
            pltpu.VMEM((FB * KA, 3 * B, 2 * B), BF16),
            pltpu.VMEM((2 * MB * B, window), BF16),
            pltpu.VMEM((2 * MB * B, window), BF16),
            halo, halo, halo, halo, halo,
            pltpu.VMEM((2, max(DETOURS), B, window), F32),
            pltpu.SMEM((MB * NX * NY,), jnp.int32),
            dma((5,)),
            dma((6,)), dma((2, NY)),
            dma((NX,)), dma((NX,)),
            dma((NX, NY)), dma((NX, NY)),
            dma((2, STEPS)), dma((2, STEPS)),
            dma((2, max(DETOURS))), dma((2, max(DETOURS))), dma((2, max(DETOURS))),
            pltpu.SemaphoreType.REGULAR((5,)),
        ],
        compiler_params=pltpu.CompilerParams(
            collective_id=0, has_side_effects=True, vmem_limit_bytes=40 * 2**20
        ),
        cost_estimate=pl.CostEstimate(flops=10**9, bytes_accessed=4 * 2**20, transcendentals=0),
        name="galerkin",
    )(*[
        pltpu.with_memory_space_constraint(each, pltpu.HBM)
        for each in (fine_blocks, prolong_blocks.reshape(FB * B, 2 * B), source_group, source_row, prolong_code.T)
    ])


def solution(mesh):
    return jax.shard_map(
        body,
        mesh=mesh,
        in_specs=(
            P(("blk", "band"), None, None),
            P(("blk", "band"), None),
            P(("blk", "band"), None),
            P(("blk", "band"), None, None),
            P(("blk", "band"), None),
        ),
        out_specs=P(("blk", "band"), None),
        check_vma=False,
    )
```

```python
import jax
import jax.numpy as jnp
from jax import lax
from jax.experimental import pallas as pl
from jax.experimental.pallas import tpu as pltpu
from jax.sharding import PartitionSpec as P

MESH = pl.DeviceIdType.MESH
F32 = jnp.float32
BF16 = jnp.bfloat16

B = 64
FB = 4
KA = 4
MB = 2
NX = 4
NY = 4
PACK = FB * B + 8
SHARE = MB * B + 8
STEPS = NX * NY // 2
DETOURS = (4, 2)
HEAD = 136


def kernel(
    a_hbm, p_hbm, group_hbm, row_hbm, code_hbm, out_ref,
    a_ref, group_ref, row_ref, code_ref,
    held, want, asked, staged, got, left_hi, left_lo, win_hi, win_lo,
    middle, up_out, down_out, lower, upper, passing, pair_tab,
    in_sem, y_send, y_recv, ask_send, ask_recv, x_send, x_recv, halo_send, halo_recv,
    pass_send, pass_recv, on_send, ready,
):
    blk, band = lax.axis_index("blk"), lax.axis_index("band")
    bands = lax.axis_size("band")
    half_bands = bands // 2
    y, x = blk // NX, blk % NX
    above, below = (band + 1) % bands, (band + bands - 1) % bands
    place = band % half_bands
    is_first, is_last = place == 0, place == half_bands - 1
    far = half_bands >= 4
    is_patient, is_passer = place == half_bands - 2, (place == half_bands - 3, place == 2)
    lane = lax.broadcasted_iota(jnp.int32, (B, 2 * B), 1)
    first_half = lane < B

    def at(row, column):
        return (row * NX + column, band)

    def inside(row):
        return (row >= 0) & (row < NY)

    def beside(shift):
        return (x + shift) % NX

    def signal(semaphore, target):
        pl.semaphore_signal(semaphore, inc=1, device_id=target, device_id_type=MESH)

    inputs = [
        pltpu.make_async_copy(source, target, in_sem.at[n])
        for n, (source, target) in enumerate((
            (group_hbm, group_ref), (row_hbm, row_ref), (code_hbm, code_ref),
            (p_hbm, held.at[y, pl.ds(0, FB * B)]), (a_hbm, a_ref),
        ))
    ]
    for copy in inputs:
        copy.start()

    barrier = pltpu.get_barrier_semaphore()
    for shift in range(1, NX):
        signal(barrier, at(y, beside(shift)))

    for jump in (1, -1, 2, -2):

        @pl.when(inside(y + jump))
        def _():
            signal(barrier, at(y + jump, x))

    @pl.when(jnp.logical_not(is_last))
    def _():
        signal(barrier, (blk, above))

    @pl.when(is_first)
    def _():
        signal(barrier, (blk, below))
        if far:
            signal(barrier, (blk, (band + bands - 3) % bands))
            signal(barrier, (blk, band + 2))

    if far:

        @pl.when(is_passer[0])
        def _():
            signal(barrier, (blk, band + 2))

        @pl.when(is_passer[1])
        def _():
            signal(barrier, (blk, (band + bands - 3) % bands))

    inputs[2].wait()
    tile_row = lax.broadcasted_iota(jnp.int32, (8, 2 * B), 0)
    tile_lane = lax.broadcasted_iota(jnp.int32, (8, 2 * B), 1)
    codes = jnp.zeros((8, 2 * B), F32)
    for i in range(FB):
        one = jnp.where(tile_lane < B, code_ref[0, i], code_ref[1, i]).astype(F32)
        codes = jnp.where(tile_row == i, one, codes)
    held[y, FB * B : PACK, :] = codes
    inputs[3].wait()

    pl.semaphore_wait(
        barrier,
        NX - 1 + sum(jnp.where(inside(y + jump), 1, 0) for jump in (1, -1, 2, -2))
        + jnp.where(is_first, 0, 1) + jnp.where(is_last, 3 if far else 1, 0)
        + (jnp.where(is_passer[0] | is_passer[1], 1, 0) if far else 0),
    )

    def y_copy(source, target, sender, part=None):
        rows = pl.ds(0, PACK) if part is None else (pl.ds(0, HEAD), pl.ds(HEAD, PACK - HEAD))[part]
        slot = held.at[source, rows]
        return pltpu.make_async_remote_copy(
            src_ref=slot, dst_ref=slot, send_sem=y_send.at[sender], recv_sem=y_recv.at[part or 0, source],
            device_id=at(target, x), device_id_type=MESH,
        )

    def ask_copy(shift):
        return pltpu.make_async_remote_copy(
            src_ref=want.at[beside(shift)], dst_ref=asked.at[NX - shift],
            send_sem=ask_send.at[shift], recv_sem=ask_recv.at[NX - shift],
            device_id=at(y, beside(shift)), device_id_type=MESH,
        )

    def x_copy(source, shift):
        return pltpu.make_async_remote_copy(
            src_ref=staged.at[shift, source], dst_ref=got.at[x, source],
            send_sem=x_send.at[shift, source], recv_sem=x_recv.at[shift, source],
            device_id=at(y, beside(shift)), device_id_type=MESH,
        )

    def x_landing(source, shift):
        return pltpu.make_async_remote_copy(
            src_ref=staged.at[shift, source], dst_ref=got.at[beside(NX - shift), source],
            send_sem=x_send.at[shift, source], recv_sem=x_recv.at[shift, source],
            device_id=at(y, beside(shift)), device_id_type=MESH,
        )

    def ask_landing(shift):
        return pltpu.make_async_remote_copy(
            src_ref=want.at[beside(shift)], dst_ref=asked.at[shift],
            send_sem=ask_send.at[shift], recv_sem=ask_recv.at[shift],
            device_id=at(y, beside(shift)), device_id_type=MESH,
        )

    def halo_copy(step, side):
        return pltpu.make_async_remote_copy(
            src_ref=(down_out if side else up_out).at[step], dst_ref=(upper if side else lower).at[step],
            send_sem=halo_send.at[side, step], recv_sem=halo_recv.at[side, step],
            device_id=(blk, below if side else above), device_id_type=MESH,
        )

    def pass_copy(side, step, n):
        return pltpu.make_async_remote_copy(
            src_ref=(down_out if side else up_out).at[step], dst_ref=passing.at[side, n],
            send_sem=pass_send.at[side, n], recv_sem=pass_recv.at[side, n],
            device_id=(blk, (band + (2 if side else bands - 2)) % bands), device_id_type=MESH,
        )

    def on_copy(side, step, n):
        return pltpu.make_async_remote_copy(
            src_ref=passing.at[side, n], dst_ref=(upper if side else lower).at[step],
            send_sem=on_send.at[side, n], recv_sem=halo_recv.at[side, step],
            device_id=(blk, (band + (bands - 3 if side else 3)) % bands), device_id_type=MESH,
        )

    order = [
        y,
        jnp.where(y == 0, 1, y - 1),
        jnp.where(y == 0, 2, jnp.where(y == 3, 1, y + 1)),
        jnp.where(y < 2, 3, 0),
    ]

    is_end = (y == 0) | (y == NY - 1)
    end_jump = jnp.where(y == 0, 1, -1)
    inner_jump = jnp.where(y == 1, 1, -1)
    hand_source, hand_target = jnp.where(y == 1, 3, 0), jnp.where(y == 1, 0, 3)

    def y_sends(act):
        @pl.when(is_end)
        def _():
            act(y_copy(y, y + 2 * end_jump, 0, 0))
            act(y_copy(y, y + 2 * end_jump, 1, 1))
            act(y_copy(y, y + end_jump, 2))

        @pl.when(jnp.logical_not(is_end))
        def _():
            act(y_copy(y, y + inner_jump, 2))
            act(y_copy(y, y - inner_jump, 3))
            act(y_copy(y, y + 2 * inner_jump, 0))

    def hand_on(part):
        return y_copy(hand_source, hand_target, 4 + part, part)

    def serve(turn):
        source = order[turn]

        def choose(wanted, slot, target):
            row = wanted(MB * source + slot)
            pick = jnp.broadcast_to(row, (B, 2 * B))
            values = jnp.zeros((B, 2 * B), F32)
            code = jnp.zeros((1, 2 * B), F32)
            for i in range(FB):
                values = jnp.where(pick == i, held[source, i * B : (i + 1) * B, :], values)
                code = jnp.where(row == i, held[source, FB * B + i : FB * B + i + 1, :], code)
            target(slice(slot * B, (slot + 1) * B), values)
            target(slice(MB * B + slot, MB * B + slot + 1), code)

        for shift in (2, 1, 3):
            for slot in range(MB):

                def wanted(n, shift=shift):
                    return asked[shift, pl.ds(n, 1), :]

                def target(rows, values, shift=shift):
                    staged[shift, source, rows, :] = values

                choose(wanted, slot, target)
            x_copy(source, shift).start()
        for slot in range(MB):

            def own(n):
                return want[x, pl.ds(n, 1), :]

            def keep(rows, values):
                got[x, source, rows, :] = values

            choose(own, slot, keep)

    def y_take(turn):
        source = order[turn]
        sender = jnp.where(source < y, y - 1, y + 1)
        if turn < 3:
            y_copy(source, sender, 0).wait_recv()
            return
        for part in range(2):
            y_copy(source, sender, 0, part).wait_recv()

            @pl.when(jnp.logical_not(is_end))
            def _():
                hand_on(part).start()

    def x_take(turn, n):
        for column in (2 * n, 2 * n + 1):
            shift = (x + NX - column) % NX

            @pl.when(shift != 0)
            def _():
                x_landing(order[turn], shift).wait_recv()

    @pl.when(jnp.logical_not(is_first))
    def _():
        signal(ready.at[0], (blk, below))

    @pl.when(is_last)
    def _():
        signal(ready.at[1], (blk, above))
        if far:
            signal(ready.at[4], (blk, (band + 3) % bands))

    if far:

        @pl.when(is_passer[1])
        def _():
            signal(ready.at[3], (blk, band - 2))

        @pl.when(is_patient)
        def _():
            pl.semaphore_wait(ready.at[2], 1)

    y_sends(lambda copy: copy.start())

    for copy in inputs[0:2]:
        copy.wait()

    def tabulate(group, carry):
        pair = [jnp.int32(0), jnp.int32(0)]
        row = [jnp.int32(FB), jnp.int32(FB)]
        for at_pair in range(FB * KA - 1, -1, -1):
            i, k = at_pair // KA, at_pair % KA
            hit = group_ref[i, k] == group
            pair = [jnp.where(hit, at_pair, pair[0]), jnp.where(hit, pair[0], pair[1])]
            row = [jnp.where(hit, row_ref[i, k], row[0]), jnp.where(hit, row[0], row[1])]
        for slot in range(MB):
            pair_tab[MB * group + slot] = pair[slot]
            want[group % NX, pl.ds(MB * (group // NX) + slot, 1), :] = jnp.full((1, 2 * B), row[slot]).astype(F32)
        return carry

    lax.fori_loop(0, NX * NY, tabulate, 0)

    for shift in (2, 1, 3):
        ask_copy(shift).start()

    def windowed(values, code, at_code):
        chosen = jnp.where(code == at_code, values, 0.0)
        return chosen + pltpu.roll(chosen, B, 1)

    def left_product(i, carry):
        p_here = held[y, pl.ds(pl.multiple_of(i * B, B), B), :]
        code = jnp.broadcast_to(held[y, pl.ds(FB * B + i, 1), :], (B, 2 * B))
        parts = [windowed(p_here, code, d) for d in range(3)]
        restrict = jnp.concatenate(
            [jnp.where(first_half, parts[0], parts[1]), jnp.where(first_half, parts[2], 0.0)], axis=1
        )
        twice = []
        for side in range(2):
            both = a_ref[i, :, side * 2 * B : (side + 1) * 2 * B]
            turned = pltpu.roll(both, B, 1)
            twice += [jnp.where(first_half, both, turned), jnp.where(first_half, turned, both)]
        result = lax.dot_general(
            restrict, jnp.concatenate(twice, axis=1), (((0,), (0,)), ((), ())),
            precision=lax.Precision.HIGHEST, preferred_element_type=F32,
        )[0 : 3 * B]
        high = result.astype(BF16)
        low = (result - high.astype(F32)).astype(BF16)
        for k in range(KA):
            left_hi[i * KA + k] = high[:, k * 2 * B : (k + 1) * 2 * B]
            left_lo[i * KA + k] = low[:, k * 2 * B : (k + 1) * 2 * B]
        return carry

    wide_half = lax.broadcasted_iota(jnp.int32, (3 * B, 2 * B), 1) < B

    def compute(step):
        for half in range(2):
            row, column = step // 2, 2 * (step % 2) + half
            for slot in range(MB):
                values = got[column, row, slot * B : (slot + 1) * B, :]
                code = jnp.broadcast_to(got[column, row, MB * B + slot : MB * B + slot + 1, :], (B, 2 * B))
                mine = first_half if half == 0 else jnp.logical_not(first_half)
                at_row = (MB * half + slot) * B
                for e in range(3):
                    part = jnp.where(mine, windowed(values, code, e), 0.0)
                    high = part.astype(BF16)
                    win_hi[at_row : at_row + B, e * 2 * B : (e + 1) * 2 * B] = high
                    win_lo[at_row : at_row + B, e * 2 * B : (e + 1) * 2 * B] = (part - high.astype(F32)).astype(BF16)

        def stacked(ref):
            pairs = [ref[pair_tab[2 * MB * step + n]] for n in range(2 * MB)]
            return jnp.concatenate(
                [jnp.where(wide_half, pairs[0], pairs[1]), jnp.where(wide_half, pairs[2], pairs[3])], axis=1
            )

        high, low = stacked(left_hi), stacked(left_lo)
        total = jnp.dot(high, win_hi[...], preferred_element_type=F32)
        total += jnp.dot(high, win_lo[...], preferred_element_type=F32)
        total += jnp.dot(low, win_hi[...], preferred_element_type=F32)
        down_out[step] = total[0:B]
        middle[step] = total[B : 2 * B]
        up_out[step] = total[2 * B : 3 * B]

    def detour(side, turn, n):
        if side == 0:
            return is_last & (n == 0), turn
        return is_first & (turn == 0), n

    def each_way(side, turn, n, act):
        step = 2 * order[turn] + n
        if not far or (side and turn):
            act(halo_copy(step, side))
            return
        around, index = detour(side, turn, n)

        @pl.when(around)
        def _():
            act(pass_copy(side, step, index))

        @pl.when(jnp.logical_not(around))
        def _():
            act(halo_copy(step, side))

    def passed_on(side, turn):
        return [(2 * order[turn], turn)] if side == 0 else [(2 * order[turn] + n, n) for n in range(2 - 2 * min(turn, 1))]

    def pass_on(side, turn):
        if far:

            @pl.when(is_passer[side])
            def _():
                if side:
                    pl.semaphore_wait(ready.at[4], 1)
                for step, index in passed_on(side, turn):
                    pass_copy(side, step, index).wait_recv()
                    on_copy(side, step, index).start()

    def finish(step):
        halo_copy(step, 0).wait_recv()
        halo_copy(step, 1).wait_recv()
        for e in range(5):
            parts = []
            for ref, shift in ((lower, 0), (middle, 1), (upper, 2)):
                if 0 <= e - shift < 3:
                    parts.append(ref[step, :, (e - shift) * 2 * B : (e - shift + 1) * 2 * B])
            column = pl.multiple_of(e * NX * NY * B + step * 2 * B, 2 * B)
            out_ref[:, pl.ds(column, 2 * B)] = sum(parts[1:], parts[0])

    def both_steps(turn, work):
        def one(n, carry):
            work(2 * order[turn] + n)
            return carry

        lax.fori_loop(0, 2, one, 0)

    def multiply(turn):
        def one(n, carry):
            x_take(turn, n)
            compute(2 * order[turn] + n)
            for side in range(2):
                each_way(side, turn, n, lambda copy: copy.start())
            return carry

        lax.fori_loop(0, 2, one, 0)

    inputs[4].wait()
    lax.fori_loop(0, 2, left_product, 0)
    for shift in range(1, NX):
        ask_landing(shift).wait_recv()
    serve(0)
    y_take(1)
    serve(1)
    y_take(2)
    serve(2)

    @pl.when(jnp.logical_not(is_end))
    def _():
        y_take(3)

    if far:

        @pl.when(is_last)
        def _():
            signal(ready.at[2], (blk, below))

    lax.fori_loop(2, FB, left_product, 0)

    @pl.when(jnp.logical_not(is_last))
    def _():
        pl.semaphore_wait(ready.at[0], 1)

    @pl.when(is_first)
    def _():
        pl.semaphore_wait(ready.at[3 if far else 1], 1)

    multiply(0)

    @pl.when(is_end)
    def _():
        y_take(3)

    serve(3)
    if far:

        @pl.when(is_first)
        def _():
            pl.semaphore_wait(ready.at[1], 1)

    pass_on(0, 0)
    multiply(1)
    pass_on(1, 0)
    pass_on(0, 1)
    multiply(2)
    pass_on(0, 2)
    pass_on(0, 3)
    multiply(3)
    for turn in range(4):
        both_steps(turn, finish)

    y_sends(lambda copy: copy.wait_send())

    @pl.when(jnp.logical_not(is_end))
    def _():
        hand_on(0).wait_send()
        hand_on(1).wait_send()

    for shift in range(1, NX):
        ask_copy(shift).wait_send()

    def drain_x(source, carry):
        for shift in range(1, NX):
            x_copy(source, shift).wait_send()
        return carry

    lax.fori_loop(0, NY, drain_x, 0)

    for side in range(2):
        for turn in range(4):
            for n in range(2):
                each_way(side, turn, n, lambda copy: copy.wait_send())
            if far and passed_on(side, turn):

                @pl.when(is_passer[side])
                def _():
                    for step, index in passed_on(side, turn):
                        on_copy(side, step, index).wait_send()


def body(fine_blocks, source_group, source_row, prolong_blocks, prolong_code):
    hbm = pl.BlockSpec(memory_space=pltpu.HBM)
    window = 3 * 2 * B
    halo = pltpu.VMEM((STEPS, B, window), F32)
    dma = pltpu.SemaphoreType.DMA
    return pl.pallas_call(
        kernel,
        out_shape=jax.ShapeDtypeStruct((B, 5 * NX * NY * B), F32),
        in_specs=[hbm] * 5,
        out_specs=pl.BlockSpec(memory_space=pltpu.VMEM),
        scratch_shapes=[
            pltpu.VMEM((FB, B, KA * B), F32),
            pltpu.SMEM((FB, KA), jnp.int32),
            pltpu.SMEM((FB, KA), jnp.int32),
            pltpu.SMEM((2, FB), jnp.int32),
            pltpu.VMEM((NY, PACK, 2 * B), F32),
            pltpu.VMEM((NX, NY * MB, 2 * B), F32),
            pltpu.VMEM((NX, NY * MB, 2 * B), F32),
            pltpu.VMEM((NX, NY, SHARE, 2 * B), F32),
            pltpu.VMEM((NX, NY, SHARE, 2 * B), F32),
            pltpu.VMEM((FB * KA, 3 * B, 2 * B), BF16),
            pltpu.VMEM((FB * KA, 3 * B, 2 * B), BF16),
            pltpu.VMEM((2 * MB * B, window), BF16),
            pltpu.VMEM((2 * MB * B, window), BF16),
            halo, halo, halo, halo, halo,
            pltpu.VMEM((2, max(DETOURS), B, window), F32),
            pltpu.SMEM((MB * NX * NY,), jnp.int32),
            dma((5,)),
            dma((6,)), dma((2, NY)),
            dma((NX,)), dma((NX,)),
            dma((NX, NY)), dma((NX, NY)),
            dma((2, STEPS)), dma((2, STEPS)),
            dma((2, max(DETOURS))), dma((2, max(DETOURS))), dma((2, max(DETOURS))),
            pltpu.SemaphoreType.REGULAR((5,)),
        ],
        compiler_params=pltpu.CompilerParams(
            collective_id=0, has_side_effects=True, vmem_limit_bytes=40 * 2**20
        ),
        cost_estimate=pl.CostEstimate(flops=10**9, bytes_accessed=4 * 2**20, transcendentals=0),
        name="galerkin",
    )(*[
        pltpu.with_memory_space_constraint(each, pltpu.HBM)
        for each in (fine_blocks, prolong_blocks.reshape(FB * B, 2 * B), source_group, source_row, prolong_code.T)
    ])


def solution(mesh):
    return jax.shard_map(
        body,
        mesh=mesh,
        in_specs=(
            P(("blk", "band"), None, None),
            P(("blk", "band"), None),
            P(("blk", "band"), None),
            P(("blk", "band"), None, None),
            P(("blk", "band"), None),
        ),
        out_specs=P(("blk", "band"), None),
        check_vma=False,
    )
```
